512 devices in a mesh: section: 16 (over y_lo, x, core), tp: 32 (over z, y_hi).
Axes of the slice: x: 4, y: 8 (y_hi: 4, y_lo: 2; y = y_hi * 2 + y_lo), z: 8, core: 2. Of those that a mesh axis runs over, the one named last changes fastest.
Arguments:
- tokens: bfloat16 [512, 8192], P('tp', 'section'), may hold values from -24 to 24, as said below
- norm_gain: float32 [8192], P('section'), may hold values from 0.5 to 1.5
- gate_weight: bfloat16 [8192, 28672], P('section', 'tp'), may hold values from -0.0625 to 0.0625
- up_weight: bfloat16 [8192, 28672], P('section', 'tp'), may hold values from -0.0625 to 0.0625
- down_weight: bfloat16 [28672, 8192], P('tp', 'section'), may hold values from -0.03125 to 0.03125
- revisit: int32 [512], P('tp'), may hold values from 1 to 2, as said below
Outputs:
- revisited: bfloat16 [512, 8192], P('tp', 'section')
The draws below stay inside these ranges and needn't reach their ends.
Inputs may be any that keep to these rules, and one draw needn't show every extreme that they name: tokens has rows and columns of different scales. Exactly 64 tokens have revisit 2; among the rows of one index of tp at most 8 do, and some index of tp has exactly 8.
All inputs are finite; a program needn't handle non-finite values.
Results may differ from the reference program's by a relative error of at most 0.017.
Values may be sent and summed in bfloat16 or wider, within the bound.
A program may use at most 64 MiB of HBM per device.

```python
import math
import jax
import jax.numpy as jnp
from jax import lax

D = 8192
FF = 28672
TOK_DEV = 16
TOKENS = 512
N_SECTION = 16
N_TP = 32


def draw_tokens(key, part):
    key = jax.random.fold_in(key, 11)
    first_key, second_key = jax.random.split(key, 2)
    columns = 10.0 ** (jnp.arange(D, dtype=jnp.float32) / D - 0.5)
    row_scale = jnp.exp(jax.random.uniform(second_key, (TOKENS, 1), jnp.float32, math.log(0.5), math.log(2.0)))
    base_values = jax.random.normal(first_key, (TOKENS, D), jnp.float32)
    return jnp.clip(base_values * row_scale * columns[None, :], -24.0, 24.0).astype(jnp.bfloat16)


def draw_revisit(key, part):
    key = jax.random.fold_in(key, 23)
    first_key, second_key = jax.random.split(key)
    holders = TOKENS // TOK_DEV
    busiest = TOK_DEV // 2
    remaining = TOKENS // 8 - busiest
    holder_ids = jnp.arange(holders - 1, dtype=jnp.int32)
    shares = (holder_ids + 1) * remaining // (holders - 1) - holder_ids * remaining // (holders - 1)
    loads = jnp.concatenate([shares, jnp.full((1,), busiest, jnp.int32)])
    loads = jax.random.permutation(first_key, loads)
    scores = jax.random.randint(second_key, (holders, TOK_DEV), 0, 1 << 20, jnp.int32) * TOK_DEV
    scores = scores + jnp.arange(TOK_DEV, dtype=jnp.int32)[None, :]
    ordering = jnp.argsort(jnp.argsort(scores, axis=1, stable=True), axis=1, stable=True).astype(jnp.int32)
    marks = (ordering < loads[:, None]).astype(jnp.int32)
    return (1 + marks).reshape(TOKENS)


def block_levels(rng, extent, cuts, low, largest):
    level, own = 1.0, jax.random.fold_in(rng, 6)
    for position, shards_of in cuts:
        heights = jnp.exp(jax.random.uniform(jax.random.fold_in(own, position), (shards_of,), jnp.float32, low / len(cuts), largest / len(cuts)))
        level = level * jnp.repeat(heights, extent[position] // shards_of).reshape([-1 if axis == position else 1 for axis in range(len(extent))])
    return level


def centred(rng, dims, deviation, reach, shards=(), held_as=jnp.bfloat16):
    gain = block_levels(rng, dims, shards, -0.22, 0.18) if shards else 1.0
    values = jax.random.normal(rng, dims, jnp.float32) * deviation * gain
    return jnp.minimum(jnp.maximum(values, -reach), reach).astype(held_as)


def setup_inputs(seed: int = 0) -> dict:
    streams_of = jax.random.split(jax.random.key(seed), 7)
    tokens = draw_tokens(jax.random.fold_in(streams_of[6], 71), 0)
    norm_gain = jnp.clip(0.5 + 1.0 * jax.random.uniform(streams_of[1], (D,), jnp.float32) ** block_levels(streams_of[1], (D,), ((0, 16),), -0.2, 0.2), 0.5, 1.5)
    gate_weight = centred(streams_of[2], (D, FF), D ** -0.5, 0.0625, ((0, 16), (1, 32)))
    up_weight = centred(streams_of[3], (D, FF), D ** -0.5, 0.0625, ((0, 16), (1, 32)))
    down_weight = centred(streams_of[4], (FF, D), FF ** -0.5, 0.03125, ((0, 32), (1, 16)))
    revisit = draw_revisit(jax.random.fold_in(streams_of[6], 71), 0)
    return {"tokens": tokens, "norm_gain": norm_gain, "gate_weight": gate_weight, "up_weight": up_weight, "down_weight": down_weight, "revisit": revisit}


def rounded(values):
    return lax.optimization_barrier(values.astype(jnp.bfloat16)).astype(jnp.float32)

def normed_rows(values, norm_gain):
    mean_sq = lax.optimization_barrier(jnp.mean(values * values, axis=1, keepdims=True))
    return values * lax.rsqrt(mean_sq + 1e-05) * norm_gain[None, :]

def block_change(normed, gate_weight, up_weight, down_weight):
    feature_width = D // N_SECTION
    gate_total = jnp.zeros((normed.shape[0], FF), jnp.float32)
    up_total = jnp.zeros((normed.shape[0], FF), jnp.float32)
    for column_block in range(N_SECTION):
        low_edge = column_block * feature_width
        high_edge = low_edge + feature_width
        segment = normed[:, low_edge:high_edge]
        gate_total = gate_total + rounded(jnp.dot(segment, gate_weight[low_edge:high_edge], preferred_element_type=jnp.float32))
        up_total = up_total + rounded(jnp.dot(segment, up_weight[low_edge:high_edge], preferred_element_type=jnp.float32))
    hidden = (jax.nn.silu(gate_total) * up_total).astype(jnp.bfloat16)
    unit_width = FF // N_TP
    change = jnp.zeros((normed.shape[0], D), jnp.float32)
    for unit_block in range(N_TP):
        low_edge = unit_block * unit_width
        high_edge = low_edge + unit_width
        change = change + rounded(jnp.dot(hidden[:, low_edge:high_edge], down_weight[low_edge:high_edge], preferred_element_type=jnp.float32))
    return change

def reference(tokens, norm_gain, gate_weight, up_weight, down_weight, revisit):
    start_state = tokens.astype(jnp.float32)
    first_normed = normed_rows(start_state, norm_gain).astype(jnp.bfloat16)
    state_one = start_state + block_change(first_normed, gate_weight, up_weight, down_weight)
    second_normed = normed_rows(state_one, norm_gain).astype(jnp.bfloat16)
    change_two = block_change(second_normed, gate_weight, up_weight, down_weight)
    again = (revisit == 2)[:, None]
    return (state_one + jnp.where(again, change_two, 0.0)).astype(jnp.bfloat16)
```

```python
import functools
import jax
import jax.numpy as jnp
from jax import lax
from jax.experimental import pallas as pl
from jax.experimental.pallas import tpu as pltpu
from jax.sharding import PartitionSpec as P

BF, F32 = jnp.bfloat16, jnp.float32
GROUPS = ((0, 256), (256, 256), (512, 256), (768, 128))
FEATURES = 8192.0
EPS = 1e-5
LAST = 99


def mo(value, unit):
    return pl.multiple_of(value, unit)


def eye(rows, lanes, offset=0):
    row = lax.broadcasted_iota(jnp.int32, (rows, lanes), 0)
    lane = lax.broadcasted_iota(jnp.int32, (rows, lanes), 1)
    return lane == row + offset


class Wire:
    def __init__(self, send_sem, recv_sem):
        self.send_sem, self.recv_sem = send_sem, recv_sem
        self.count, self.sent = 0, []

    def slot(self):
        self.count += 1
        return self.count - 1

    def send(self, src, dst, slot, dev):
        copy = pltpu.make_async_remote_copy(
            src_ref=src, dst_ref=dst, send_sem=self.send_sem.at[slot], recv_sem=self.recv_sem.at[slot],
            device_id=dev, device_id_type=pl.DeviceIdType.MESH)
        copy.start()
        self.sent.append(copy)

    def recv(self, dst, slot, dev):
        pltpu.make_async_remote_copy(
            src_ref=dst, dst_ref=dst, send_sem=self.send_sem.at[slot], recv_sem=self.recv_sem.at[slot],
            device_id=dev, device_id_type=pl.DeviceIdType.MESH).wait_recv()

    def drain(self):
        for copy in self.sent:
            copy.wait_send()


def kernel(upto, tok, gain, rev_row, rev_col, wg, wu, wd, out,
           X, XG, W, WD, F, snd, own, crecv, fwdp, fwdm, dirp, dirm, ysnd, yrecv, tot, H,
           D, upb, dnb, tsum, tbf, yb, SS, SSr, S2, S2r,
           X2, C, G2, c2r, x2r, y2s, y2r, t2, H2, D2, upb2, dnb2, tsum2, tbf2, yb2, st,
           wsem, send_sem, recv_sem):
    s, t = lax.axis_index("section"), lax.axis_index("tp")
    c, x, yl = s % 2, (s // 2) % 4, s // 8
    z, yh = t // 4, t % 4
    wire = Wire(send_sem, recv_sem)

    def sec(dc=0, dx=0, dy=0):
        return ((((yl + dy) % 2) * 4 + (x + dx) % 4) * 2 + (c + dc) % 2, t)

    def tpd(dz=0, dh=0):
        return (s, ((z + dz + 8) % 8) * 4 + (yh + dh) % 4)

    core, ydev = sec(dc=1), sec(dy=1)
    xs = {j: sec(dx=j) for j in (1, 2, 3)}
    ups, downs = tpd(dz=1), tpd(dz=-1)
    yhs = {j: tpd(dh=j) for j in (1, 2, 3)}

    barrier = pltpu.get_barrier_semaphore()
    peers = [core, ydev, ups, downs] + list(xs.values()) + list(yhs.values())
    for peer in peers:
        pl.semaphore_signal(barrier, inc=1, device_id=peer, device_id_type=pl.DeviceIdType.MESH)

    loads = []
    for g, (lo, w) in enumerate(GROUPS):
        loads.append(pltpu.make_async_copy(wg.at[:, lo:lo + w], W.at[:, 2 * lo:2 * lo + w], wsem.at[2 * g]))
        loads.append(pltpu.make_async_copy(wu.at[:, lo:lo + w], W.at[:, 2 * lo + w:2 * lo + 2 * w], wsem.at[2 * g + 1]))
    load_down = pltpu.make_async_copy(wd, WD, wsem.at[8])
    for load in loads:
        load.start()
    load_down.start()
    X[pl.ds(mo(t * 16, 16), 16), :] = tok[...]
    flag_row = jnp.where(rev_row[...] == 2, 1.0, 0.0)
    F[t] = jnp.concatenate([flag_row, jnp.zeros((1, 112), F32)], axis=1)
    pl.semaphore_wait(barrier, len(peers))

    def finish():
        wire.drain()

    def ring_gather(buf, flags):
        def rows(zz, j):
            return buf.at[pl.ds(mo(((((zz + 16) % 8) * 4) + (yh - j + 4) % 4) * 16, 16), 16), :]

        def frow(zz):
            return flags.at[pl.ds(((zz + 16) % 8) * 4, 4)]

        yslot = {j: wire.slot() for j in (1, 2, 3)}
        uslot = {(k, j): wire.slot() for k in range(4) for j in range(4)}
        dslot = {(k, j): wire.slot() for k in range(4) for j in range(4)}
        order = (0, 1, 3, 2)
        mine = rows(z, 0)
        wire.send(mine, mine, uslot[0, 0], ups)
        wire.send(mine, mine, dslot[0, 0], downs)
        for j in (1, 3, 2):
            wire.send(mine, mine, yslot[j], yhs[j])
        if flags is not None:
            fy = {j: wire.slot() for j in (1, 2, 3)}
            for j in (1, 2, 3):
                wire.send(flags.at[pl.ds(t, 1)], flags.at[pl.ds(t, 1)], fy[j], yhs[j])
        for k in range(4):
            for j in order:
                if k == 0:
                    if j == 0:
                        continue
                    wire.recv(rows(z, j), yslot[j], yhs[j])
                    wire.send(rows(z, j), rows(z, j), uslot[k, j], ups)
                    wire.send(rows(z, j), rows(z, j), dslot[k, j], downs)
                    continue
                wire.recv(rows(z - k, j), uslot[k - 1, j], downs)
                if k < 3 or j in (0, 1):
                    wire.send(rows(z - k, j), rows(z - k, j), uslot[k, j], ups)
                wire.recv(rows(z + k, j), dslot[k - 1, j], ups)
                if k < 3 or j in (2, 3):
                    wire.send(rows(z + k, j), rows(z + k, j), dslot[k, j], downs)
        for j in (0, 1):
            wire.recv(rows(z - 4, j), uslot[3, j], downs)
        for j in (3, 2):
            wire.recv(rows(z + 4, j), dslot[3, j], ups)
        if flags is None:
            return None

        def step(k):
            if k == 0:
                for j in (1, 2, 3):
                    wire.recv(flags.at[pl.ds(z * 4 + (yh - j + 4) % 4, 1)], fy[j], yhs[j])
            else:
                wire.recv(frow(z - k), step.up[k - 1], downs)
                if k < 4:
                    wire.recv(frow(z + k), step.down[k - 1], ups)
            if k < 4:
                step.up[k] = wire.slot()
                wire.send(frow(z - k), frow(z - k), step.up[k], ups)
            if k < 3:
                step.down[k] = wire.slot()
                wire.send(frow(z + k), frow(z + k), step.down[k], downs)
        step.up, step.down = {}, {}
        return step

    def ring_reduce(src, ub, db, ts, tb, ybuf, block_done):
        def part(off, h):
            return src.at[pl.ds(mo(((z + off + 8) % 8) * 64 + h * 32, 32), 32), :]

        us = {(k, h): wire.slot() for k in range(4) for h in range(2)}
        ds = {(k, h): wire.slot() for k in range(4) for h in range(2)}
        block_done(4)
        wire.send(part(4, 0), ub.at[0, 0:32, :], us[0, 0], ups)
        wire.send(part(4, 1), db.at[0, 32:64, :], ds[0, 1], downs)
        for k in (1, 2, 3):
            block_done(4 - k)
            for h in ((1, 0) if k == 1 else (0, 1)):
                hu, hd = h, 1 - h
                if k > 1 or hu == 0:
                    got = ub.at[k - 1, hu * 32:hu * 32 + 32, :]
                    wire.recv(got, us[k - 1, hu], downs)
                    mine = part(4 - k, hu)
                    mine[...] = (mine[...].astype(F32) + got[...].astype(F32)).astype(BF)
                wire.send(part(4 - k, hu), ub.at[k, hu * 32:hu * 32 + 32, :], us[k, hu], ups)
                if k > 1 or hd == 1:
                    got = db.at[k - 1, hd * 32:hd * 32 + 32, :]
                    wire.recv(got, ds[k - 1, hd], ups)
                    mine = part(k - 4, hd)
                    mine[...] = (mine[...].astype(F32) + got[...].astype(F32)).astype(BF)
                wire.send(part(k - 4, hd), db.at[k, hd * 32:hd * 32 + 32, :], ds[k, hd], downs)
        for h in (0, 1):
            a, b = ub.at[3, h * 32:h * 32 + 32, :], db.at[3, h * 32:h * 32 + 32, :]
            wire.recv(a, us[3, h], downs)
            wire.recv(b, ds[3, h], ups)
            total = part(0, h)[...].astype(F32) + a[...].astype(F32) + b[...].astype(F32)
            ts[h * 32:h * 32 + 32, :] = total
            tb[h * 32:h * 32 + 32, :] = total.astype(BF)
        ys = {j: wire.slot() for j in (1, 2, 3)}
        for j in (2, 1, 3):
            wire.send(tb.at[pl.ds(mo(((yh + j) % 4) * 16, 16), 16), :], ybuf.at[j - 1], ys[j], yhs[j])
        total = ts[pl.ds(mo(yh * 16, 16), 16), :]
        for j in (1, 3, 2):
            wire.recv(ybuf.at[j - 1], ys[j], yhs[j])
            total = total + ybuf[j - 1].astype(F32)
        return total

    fstep = ring_gather(X, F)
    if upto < 1:
        for k in range(5):
            fstep(k)
        out[...] = X[pl.ds(mo(t * 16, 16), 16), :]
        return finish()

    g = gain[...]
    for b in range(4):
        part_cols = []
        for q in range(4):
            lo = b * 128 + q * 32
            v = X[lo:lo + 32, :].astype(F32)
            XG[lo:lo + 32, :] = (v * g).astype(BF)
            part_cols.append(jnp.sum(v * v, axis=1, keepdims=True))
        col = jnp.concatenate(part_cols, axis=0)
        SS[b:b + 1, :] = jnp.sum(jnp.where(eye(128, 128), col, 0.0), axis=0, keepdims=True)
    SS[4:8, :] = jnp.zeros((4, 128), F32)

    def sq_rounds(ss, rr):
        slots = [wire.slot() for _ in range(5)]

        def start(n):
            if n == 0:
                wire.send(ss, rr.at[0], slots[0], core)
            if n == 1:
                wire.recv(rr.at[0], slots[0], core)
                ss2 = rr.at[5]
                ss2[...] = ss[...] + rr[0]
                for j in (1, 2, 3):
                    wire.send(ss2, rr.at[j], slots[j], xs[j])
            if n == 2:
                for j in (1, 2, 3):
                    wire.recv(rr.at[j], slots[j], xs[j])
                ss3 = rr.at[6]
                ss3[...] = rr[5] + rr[1] + rr[2] + rr[3]
                wire.send(ss3, rr.at[4], slots[4], ydev)
            if n == 3:
                wire.recv(rr.at[4], slots[4], ydev)
                rr[7] = rr[6] + rr[4]
        return start

    sq = sq_rounds(SS, SSr)
    sq(0)

    def gate_up(row0, g_index, dst):
        lo, w = GROUPS[g_index]

        @pl.loop(0, 2)
        def _(i):
            r = mo(i * 128, 128)
            dst[pl.ds(r, 128), 2 * lo:2 * lo + 2 * w] = jnp.dot(
                XG[pl.ds(mo(row0 + r, 128), 128), :], W[:, 2 * lo:2 * lo + 2 * w],
                preferred_element_type=F32).astype(BF)

    def cols(g_index):
        lo, w = GROUPS[g_index]
        return slice(2 * lo, 2 * lo + 2 * w)

    NG = len(GROUPS)
    cslot = [wire.slot() for _ in range(NG)]
    for p in range(NG):
        loads[2 * p].wait()
        loads[2 * p + 1].wait()
        gate_up((1 - c) * 256, p, snd)
        wire.send(snd.at[:, cols(p)], crecv.at[:, cols(p)], cslot[p], core)
    for k in range(5):
        fstep(k)

    def blk(off, h):
        return pl.ds(mo(((x + off) % 4) * 64 + h * 32, 32), 32)

    xslot = [[wire.slot() for _ in range(6)] for _ in range(NG)]
    for p in range(NG):
        gate_up(c * 256, p, own)
        wire.recv(crecv.at[:, cols(p)], cslot[p], core)

        @pl.loop(0, 8)
        def _(i):
            r = pl.ds(mo(i * 32, 32), 32)
            own[r, cols(p)] = (own[r, cols(p)].astype(F32) + crecv[r, cols(p)].astype(F32)).astype(BF)
        wire.send(own.at[blk(2, 0), cols(p)], fwdp.at[:, cols(p)], xslot[p][0], xs[1])
        wire.send(own.at[blk(2, 1), cols(p)], fwdm.at[:, cols(p)], xslot[p][1], xs[3])
        wire.send(own.at[blk(1, 1), cols(p)], dirp.at[32:64, cols(p)], xslot[p][2], xs[1])
        wire.send(own.at[blk(3, 0), cols(p)], dirm.at[0:32, cols(p)], xslot[p][3], xs[3])
        if p == 0:
            sq(1)
    if upto < 2:
        for p in range(NG):
            wire.recv(fwdp.at[:, cols(p)], xslot[p][0], xs[3])
            wire.recv(fwdm.at[:, cols(p)], xslot[p][1], xs[1])
            wire.recv(dirp.at[32:64, cols(p)], xslot[p][2], xs[3])
            wire.recv(dirm.at[0:32, cols(p)], xslot[p][3], xs[1])
        sq(2)
        sq(3)
        load_down.wait()
        out[...] = own[0:16, 0:512] + fwdp[0:16, 0:512]
        return finish()
    for p in range(NG):
        wire.recv(fwdp.at[:, cols(p)], xslot[p][0], xs[3])
        r = blk(1, 0)
        own[r, cols(p)] = (own[r, cols(p)].astype(F32) + fwdp[:, cols(p)].astype(F32)).astype(BF)
        wire.send(own.at[r, cols(p)], dirp.at[0:32, cols(p)], xslot[p][4], xs[1])
        wire.recv(fwdm.at[:, cols(p)], xslot[p][1], xs[1])
        r = blk(3, 1)
        own[r, cols(p)] = (own[r, cols(p)].astype(F32) + fwdm[:, cols(p)].astype(F32)).astype(BF)
        wire.send(own.at[r, cols(p)], dirm.at[32:64, cols(p)], xslot[p][5], xs[3])
    sq(2)
    yslot = [wire.slot() for _ in range(NG)]
    mine, other = yl, 1 - yl
    for p in range(NG):
        wire.recv(dirp.at[32:64, cols(p)], xslot[p][2], xs[3])
        wire.recv(dirm.at[0:32, cols(p)], xslot[p][3], xs[1])
        wire.recv(dirp.at[0:32, cols(p)], xslot[p][4], xs[3])
        wire.recv(dirm.at[32:64, cols(p)], xslot[p][5], xs[1])

        def xsum(h):
            hr = pl.ds(mo(h * 32, 32), 32)
            return (own[blk(0, h), cols(p)].astype(F32) + dirp[hr, cols(p)].astype(F32)
                    + dirm[hr, cols(p)].astype(F32))
        ysnd[:, cols(p)] = xsum(other).astype(BF)
        wire.send(ysnd.at[:, cols(p)], yrecv.at[:, cols(p)], yslot[p], ydev)
        tot[:, cols(p)] = xsum(mine)
    sq(3)
    row0 = c * 256 + x * 64 + yl * 32

    def scale_of(rr, first, count):
        line = rr[7, pl.ds(first // 128, 1), :]
        picked = jnp.where(eye(count, 128, first % 128), line, 0.0)
        return lax.rsqrt(jnp.sum(picked, axis=1, keepdims=True) / FEATURES + EPS)

    scale = scale_of(SSr, row0, 32)

    def act(gate, up):
        return (gate / (1.0 + jnp.exp(-gate)) * up).astype(BF)

    def hrows(off, h):
        return pl.ds(mo(c * 256 + ((x + off) % 4) * 64 + h * 32, 32), 32)

    hy = [wire.slot() for _ in range(NG)]
    hx = [[wire.slot() for _ in range(6)] for _ in range(NG)]
    hc = [wire.slot() for _ in range(NG)]

    def hcols(p):
        lo, w = GROUPS[p]
        return slice(lo, lo + w)

    def hsend(off, h, p, slot, dev):
        ref = H.at[hrows(off, h), hcols(p)]
        wire.send(ref, ref, slot, dev)

    def hrecv(off, h, p, slot, dev):
        wire.recv(H.at[hrows(off, h), hcols(p)], slot, dev)

    for p in range(NG):
        lo, w = GROUPS[p]
        wire.recv(yrecv.at[:, cols(p)], yslot[p], ydev)
        gate = (tot[:, 2 * lo:2 * lo + w] + yrecv[:, 2 * lo:2 * lo + w].astype(F32)) * scale
        up = (tot[:, 2 * lo + w:2 * lo + 2 * w] + yrecv[:, 2 * lo + w:2 * lo + 2 * w].astype(F32)) * scale
        H[hrows(0, mine), hcols(p)] = act(gate, up)
        hsend(0, mine, p, hy[p], ydev)
        hsend(0, mine, p, hx[p][0], xs[1])
        hsend(0, mine, p, hx[p][1], xs[3])
    if upto < 3:
        for p in range(NG):
            hrecv(0, other, p, hy[p], ydev)
            hrecv(3, mine, p, hx[p][0], xs[3])
            hrecv(1, mine, p, hx[p][1], xs[1])
        load_down.wait()
        out[...] = H[0:16, 0:512]
        return finish()
    for p in range(NG):
        hrecv(0, other, p, hy[p], ydev)
        hsend(0, other, p, hx[p][2], xs[1])
        hsend(0, other, p, hx[p][3], xs[3])
        hrecv(3, mine, p, hx[p][0], xs[3])
        hsend(3, mine, p, hx[p][4], xs[1])
        hrecv(1, mine, p, hx[p][1], xs[1])
    for p in range(NG):
        hrecv(3, other, p, hx[p][2], xs[3])
        hrecv(1, other, p, hx[p][3], xs[1])
        hsend(1, other, p, hx[p][5], xs[3])
    for p in range(NG):
        hrecv(2, mine, p, hx[p][4], xs[3])
        hrecv(2, other, p, hx[p][5], xs[1])
        half = H.at[pl.ds(mo(c * 256, 256), 256), hcols(p)]
        wire.send(half, half, hc[p], core)
    for p in range(NG):
        wire.recv(H.at[pl.ds(mo((1 - c) * 256, 256), 256), hcols(p)], hc[p], core)
    load_down.wait()
    if upto < 4:
        out[...] = H[0:16, 0:512]
        return finish()

    def down_pair(off):
        a = pl.ds(mo(((z + off) % 8) * 64, 64), 64)
        b = pl.ds(mo(((z - off + 8) % 8) * 64, 64), 64)
        if off == 4:
            b = pl.ds(mo(z * 64, 64), 64)
        rows = jnp.concatenate([H[a, :], H[b, :]], axis=0)
        prod = jnp.dot(rows, WD[...], preferred_element_type=F32).astype(BF)
        D[a, :] = prod[0:64]
        D[b, :] = prod[64:128]

    delta = ring_reduce(D, upb, dnb, tsum, tbf, yb, down_pair)
    state = tok[...].astype(F32) + delta
    st[...] = state
    if upto < 5:
        out[...] = state.astype(BF)
        return finish()

    active_row = rev_row[...] == 2
    active_col = rev_col[...] == 2
    sub = lax.broadcasted_iota(jnp.int32, (16, 16), 0)
    lane = lax.broadcasted_iota(jnp.int32, (16, 16), 1)
    place_row = jnp.sum(jnp.where((sub <= lane) & active_col, 1, 0), axis=0, keepdims=True) - 1
    place_col = jnp.sum(jnp.where((lane <= sub) & active_row, 1, 0), axis=1, keepdims=True) - 1
    picks = jnp.where((sub % 8 == place_row) & active_row, 1.0, 0.0).astype(BF)
    picked = jnp.dot(picks, (state * g).astype(BF), preferred_element_type=F32)
    fold = lax.broadcasted_iota(jnp.int32, (16, 256), 0) < 8
    X2[pl.ds(mo(t * 16, 16), 16), :] = jnp.where(fold, picked[:, 0:256], picked[:, 256:512]).astype(BF)
    ring_gather(X2, None)
    if upto < 6:
        out[...] = X2[0:16, :][:, 0:1].astype(F32).astype(BF) + state.astype(BF)
        return finish()

    counts = jnp.sum(F[...].reshape(32, 128), axis=1, keepdims=True)
    owner = lax.broadcasted_iota(jnp.int32, (32, 512), 1) // 16
    unit = lax.broadcasted_iota(jnp.int32, (32, 512), 0)
    before = jnp.sum(jnp.where(unit < owner, counts, 0.0), axis=0, keepdims=True)
    here = jnp.sum(jnp.where(unit == owner, counts, 0.0), axis=0, keepdims=True)
    slot_lane = lax.broadcasted_iota(jnp.int32, (1, 512), 1) % 16
    place = (slot_lane % 8).astype(F32)
    goal = jnp.where(place < here, before + place, -1.0)
    want = lax.broadcasted_iota(jnp.int32, (64, 512), 0).astype(F32)
    hit = jnp.where(goal == want, 1.0, 0.0)
    left = jnp.where(slot_lane < 8, hit, 0.0).astype(BF)
    right = jnp.where(slot_lane >= 8, hit, 0.0).astype(BF)
    C[:, 0:256] = jnp.dot(left, X2[...], preferred_element_type=F32).astype(BF)
    C[:, 256:512] = jnp.dot(right, X2[...], preferred_element_type=F32).astype(BF)
    unscaled = C[...].astype(F32) / g
    col = jnp.sum(unscaled * unscaled, axis=1, keepdims=True)
    S2[...] = jnp.zeros((8, 128), F32)
    S2[0:1, :] = jnp.sum(jnp.where(eye(64, 128), col, 0.0), axis=0, keepdims=True)
    sq2 = sq_rounds(S2, S2r)
    sq2(0)
    for p in range(NG):
        lo, w = GROUPS[p]
        prod = jnp.dot(C[...], W[:, cols(p)], preferred_element_type=F32).astype(BF)
        G2[:, 512 * p:512 * p + w] = prod[:, 0:w]
        G2[:, 512 * p + 256:512 * p + 256 + w] = prod[:, w:2 * w]
        if w < 256:
            G2[:, 512 * p + w:512 * p + 256] = jnp.zeros((64, 256 - w), BF)
            G2[:, 512 * p + 256 + w:512 * p + 512] = jnp.zeros((64, 256 - w), BF)
    slot = wire.slot()
    wire.send(G2.at[pl.ds(mo((1 - c) * 32, 32), 32), :], c2r, slot, core)
    mine_rows = pl.ds(mo(c * 32, 32), 32)
    wire.recv(c2r, slot, core)
    G2[mine_rows, :] = (G2[mine_rows, :].astype(F32) + c2r[...].astype(F32)).astype(BF)
    slots = {j: wire.slot() for j in (1, 2, 3)}
    for j in (2, 1, 3):
        wire.send(G2.at[mine_rows, pl.ds(mo(((x + j) % 4) * 512, 512), 512)], x2r.at[j - 1], slots[j], xs[j])
    sq2(1)
    for j in (1, 2, 3):
        wire.recv(x2r.at[j - 1], slots[j], xs[j])
    sum2 = G2[mine_rows, pl.ds(mo(x * 512, 512), 512)].astype(F32)
    for j in (1, 2, 3):
        sum2 = sum2 + x2r[j - 1].astype(F32)
    t2[...] = sum2
    y2s[...] = sum2.astype(BF)
    slot = wire.slot()
    wire.send(y2s.at[pl.ds(mo(other * 16, 16), 16), :], y2r, slot, ydev)
    sq2(2)
    sq2(3)
    scale2 = scale_of(S2r, c * 32 + yl * 16, 16)
    wire.recv(y2r, slot, ydev)
    full = (t2[pl.ds(mo(mine * 16, 16), 16), :] + y2r[...].astype(F32)) * scale2

    def h2(yy, xx):
        return H2.at[pl.ds(mo(c * 32 + yy * 16, 16), 16), pl.ds(mo(xx * 256, 256), 256)]

    h2(mine, x)[...] = act(full[:, 0:256], full[:, 256:512])
    slot = wire.slot()
    wire.send(h2(mine, x), h2(mine, x), slot, ydev)
    slots = {(j, h): wire.slot() for j in (1, 2, 3) for h in (0, 1)}
    for j in (2, 1, 3):
        wire.send(h2(mine, x), h2(mine, x), slots[j, 0], xs[j])
    wire.recv(h2(other, x), slot, ydev)
    for j in (2, 1, 3):
        wire.send(h2(other, x), h2(other, x), slots[j, 1], xs[j])
    for j in (1, 2, 3):
        wire.recv(h2(mine, (x + 4 - j) % 4), slots[j, 0], xs[j])
        wire.recv(h2(other, (x + 4 - j) % 4), slots[j, 1], xs[j])
    slot = wire.slot()
    wire.send(H2.at[mine_rows, :], H2.at[mine_rows, :], slot, core)
    wire.recv(H2.at[pl.ds(mo((1 - c) * 32, 32), 32), :], slot, core)
    if upto < 7:
        out[...] = H2[0:16, 0:512]
        return finish()
    down2 = jnp.dot(H2[:, 0:896], WD[...], preferred_element_type=F32).astype(BF)
    spread = (((0,), (0,)), ((), ()))
    D2[...] = (lax.dot_general(left, down2[:, 0:256], spread, preferred_element_type=F32)
               + lax.dot_general(right, down2[:, 256:512], spread, preferred_element_type=F32)).astype(BF)
    back = ring_reduce(D2, upb2, dnb2, tsum2, tbf2, yb2, lambda off: None)
    acc_l = jnp.zeros((16, 256), F32)
    acc_r = jnp.zeros((16, 256), F32)
    for k in range(8):
        put = jnp.where((place_col == k) & active_col, 1.0, 0.0)
        acc_l = acc_l + put * back[k:k + 1, :]
        acc_r = acc_r + put * back[k + 8:k + 9, :]
    out[...] = (st[...] + jnp.concatenate([acc_l, acc_r], axis=1)).astype(BF)
    finish()


def body(upto, tokens, norm_gain, gate_weight, up_weight, down_weight, revisit):
    vm = lambda *shape: pltpu.VMEM(shape, BF)
    vf = lambda *shape: pltpu.VMEM(shape, F32)
    vspec, anyspec = pl.BlockSpec(memory_space=pltpu.VMEM), pl.BlockSpec(memory_space=pl.ANY)
    scratch = [
        vm(512, 512), vm(512, 512), vm(512, 1792), vm(896, 512), vf(32, 1, 128),
        vm(256, 1792), vm(256, 1792), vm(256, 1792), vm(32, 1792), vm(32, 1792), vm(64, 1792), vm(64, 1792),
        vm(32, 1792), vm(32, 1792), vf(32, 1792), vm(512, 896),
        vm(512, 512), vm(4, 64, 512), vm(4, 64, 512), vf(64, 512), vm(64, 512), vm(3, 16, 512),
        vf(8, 128), vf(8, 8, 128), vf(8, 128), vf(8, 8, 128),
        vm(512, 256), vm(64, 512), vm(64, 2048), vm(32, 2048), vm(3, 32, 512), vm(32, 512), vm(16, 512), vf(32, 512),
        vm(64, 1024), vm(512, 256), vm(4, 64, 256), vm(4, 64, 256), vf(64, 256), vm(64, 256), vm(3, 16, 256),
        vf(16, 512),
        pltpu.SemaphoreType.DMA((9,)), pltpu.SemaphoreType.DMA((260,)), pltpu.SemaphoreType.DMA((260,)),
    ]
    return pl.pallas_call(
        functools.partial(kernel, upto),
        out_shape=jax.ShapeDtypeStruct((16, 512), BF),
        in_specs=[vspec] * 4 + [anyspec] * 3,
        out_specs=vspec,
        scratch_shapes=scratch,
        compiler_params=pltpu.CompilerParams(
            collective_id=0, has_side_effects=True, vmem_limit_bytes=40 * 1024 * 1024),
        cost_estimate=pl.CostEstimate(flops=2000000000, bytes_accessed=3000000, transcendentals=30000),
        name="two_pass_block",
    )(tokens, norm_gain.reshape(1, 512), revisit.reshape(1, 16), revisit.reshape(16, 1),
      gate_weight, up_weight, down_weight)


def solution(mesh, upto=LAST):
    placed = (P("tp", "section"), P("section"), P("section", "tp"), P("section", "tp"), P("tp", "section"), P("tp"))
    return jax.shard_map(functools.partial(body, upto), mesh=mesh, in_specs=placed,
                         out_specs=P("tp", "section"), check_vma=False)
```

```python
import functools
import jax
import jax.numpy as jnp
from jax import lax
from jax.experimental import pallas as pl
from jax.experimental.pallas import tpu as pltpu
from jax.sharding import PartitionSpec as P

BF, F32 = jnp.bfloat16, jnp.float32
GROUPS = ((0, 256), (256, 256), (512, 256), (768, 128))
FEATURES = 8192.0
EPS = 1e-5
LAST = 99


def mo(value, unit):
    return pl.multiple_of(value, unit)


def eye(rows, lanes, offset=0):
    row = lax.broadcasted_iota(jnp.int32, (rows, lanes), 0)
    lane = lax.broadcasted_iota(jnp.int32, (rows, lanes), 1)
    return lane == row + offset


class Wire:
    def __init__(self, send_sem, recv_sem):
        self.send_sem, self.recv_sem = send_sem, recv_sem
        self.count, self.sent = 0, []

    def slot(self):
        self.count += 1
        return self.count - 1

    def send(self, src, dst, slot, dev):
        copy = pltpu.make_async_remote_copy(
            src_ref=src, dst_ref=dst, send_sem=self.send_sem.at[slot], recv_sem=self.recv_sem.at[slot],
            device_id=dev, device_id_type=pl.DeviceIdType.MESH)
        copy.start()
        self.sent.append(copy)

    def recv(self, dst, slot, dev):
        pltpu.make_async_remote_copy(
            src_ref=dst, dst_ref=dst, send_sem=self.send_sem.at[slot], recv_sem=self.recv_sem.at[slot],
            device_id=dev, device_id_type=pl.DeviceIdType.MESH).wait_recv()

    def drain(self):
        for copy in self.sent:
            copy.wait_send()


def kernel(upto, tok, gain, rev, wg, wu, wd, out,
           X, XG, W, WD, F, GN, RV, snd, own, crecv, fwdp, fwdm, dirp, dirm, ysnd, yrecv, tot, H,
           D, upb, dnb, tsum, tbf, yb, SS, SSr, S2, S2r, TRI, SPR,
           XF, C, G2, c2r, x2r, H2, PF, zr, z3, yex, ZA, D2, upb2, dnb2, tsum2, tbf2, yb2, st,
           wsem, send_sem, recv_sem):
    s, t = lax.axis_index("section"), lax.axis_index("tp")
    c, x, yl = s % 2, (s // 2) % 4, s // 8
    z, yh = t // 4, t % 4
    wire = Wire(send_sem, recv_sem)
    mine, other = yl, 1 - yl

    def sec(dc=0, dx=0, dy=0):
        return ((((yl + dy + 2) % 2) * 4 + (x + dx + 4) % 4) * 2 + (c + dc) % 2, t)

    def tpd(dz=0, dh=0):
        return (s, ((z + dz + 8) % 8) * 4 + (yh + dh + 4) % 4)

    core, ydev = sec(dc=1), sec(dy=1)
    xs = {j: sec(dx=j) for j in (1, 2, 3)}
    zs = {j: tpd(dz=j) for j in range(1, 8)}
    ups, downs = zs[1], zs[7]
    yhs = {j: tpd(dh=j) for j in (1, 2, 3)}
    around = [(2, 1), (2, 0), (1, 1), (3, 1), (1, 0), (3, 0), (0, 1)]
    xys = [sec(dx=a, dy=b) for a, b in around]

    loads = []
    for g, (lo, w) in enumerate(GROUPS):
        loads.append(pltpu.make_async_copy(wg.at[:, lo:lo + w], W.at[:, 2 * lo:2 * lo + w], wsem.at[2 * g]))
        loads.append(pltpu.make_async_copy(wu.at[:, lo:lo + w], W.at[:, 2 * lo + w:2 * lo + 2 * w], wsem.at[2 * g + 1]))
    load_down = pltpu.make_async_copy(wd, WD, wsem.at[8])
    my_rows = pl.ds(mo(t * 16, 16), 16)
    small = [pltpu.make_async_copy(tok, X.at[my_rows, :], wsem.at[9]), pltpu.make_async_copy(rev, RV, wsem.at[10]),
             pltpu.make_async_copy(gain, GN, wsem.at[11])]
    for load in small + loads + [load_down]:
        load.start()

    barrier = pltpu.get_barrier_semaphore()
    peers = [core] + list(zs.values()) + list(yhs.values()) + xys
    for peer in peers:
        pl.semaphore_signal(barrier, inc=1, device_id=peer, device_id_type=pl.DeviceIdType.MESH)
    TRI[...] = jnp.where(lax.broadcasted_iota(jnp.int32, (512, 512), 0)
                         <= lax.broadcasted_iota(jnp.int32, (512, 512), 1), 1.0, 0.0).astype(BF)
    SPR[...] = jnp.where(lax.broadcasted_iota(jnp.int32, (128, 512), 1) % 16
                         == lax.broadcasted_iota(jnp.int32, (128, 512), 0), 1.0, 0.0).astype(BF)
    for load in small:
        load.wait()
    flag_row = jnp.where(RV[...] == 2, 1.0, 0.0)
    F[t] = jnp.concatenate([flag_row, jnp.zeros((1, 112), F32)], axis=1)
    pl.semaphore_wait(barrier, len(peers))
    done = object()

    def finish():
        wire.drain()

    def rows(dz, j):
        return X.at[pl.ds(mo(((z + dz + 8) % 8) * 64 + ((yh - j + 4) % 4) * 16, 16), 16), :]

    def frow(dz):
        return F.at[pl.ds(((z + dz + 8) % 8) * 4, 4)]

    def same(ref, slot, dev):
        wire.send(ref, ref, slot, dev)

    fy = {j: wire.slot() for j in (1, 2, 3)}
    fz = {d: wire.slot() for d in range(1, 8)}
    sy = {j: wire.slot() for j in (1, 2, 3)}
    sz = {(d, j): wire.slot() for d in range(1, 8) for j in range(4)}
    for j in (2, 1, 3):
        same(F.at[pl.ds(t, 1)], fy[j], yhs[j])
        same(rows(0, 0), sy[j], yhs[j])

    def spread(j):
        for d in (2, 6, 1, 7):
            same(rows(0, j), sz[d, j], zs[d])

    def relay(j):
        wire.recv(rows(-2, j), sz[2, j], zs[6])
        if j in (0, 1):
            same(rows(-2, j), sz[4, j], zs[2])
        same(rows(-2, j), sz[3, j], zs[1])
        wire.recv(rows(2, j), sz[6, j], zs[2])
        if j in (2, 3):
            same(rows(2, j), sz[4, j], zs[6])
        same(rows(2, j), sz[5, j], zs[7])

    def take(j):
        wire.recv(rows(-1, j), sz[1, j], zs[7])
        wire.recv(rows(1, j), sz[7, j], zs[1])
        wire.recv(rows(-3, j), sz[3, j], zs[7])
        wire.recv(rows(3, j), sz[5, j], zs[1])
        wire.recv(rows(4, j), sz[4, j], zs[6] if j in (0, 1) else zs[2])

    spread(0)
    for j in (1, 3):
        wire.recv(rows(0, j), sy[j], yhs[4 - j])
        spread(j)
    relay(0)
    for j in (1, 2, 3):
        wire.recv(F.at[pl.ds(z * 4 + (yh - j + 4) % 4, 1)], fy[j], yhs[4 - j])
    for d in (2, 6, 1, 7):
        same(frow(0), fz[d], zs[d])
    wire.recv(rows(0, 2), sy[2], yhs[2])
    spread(2)
    relay(1)
    relay(3)
    wire.recv(frow(-2), fz[2], zs[6])
    same(frow(-2), fz[4], zs[2])
    same(frow(-2), fz[3], zs[1])
    wire.recv(frow(2), fz[6], zs[2])
    same(frow(2), fz[5], zs[7])
    relay(2)
    wire.recv(frow(-1), fz[1], zs[7])
    wire.recv(frow(1), fz[7], zs[1])
    wire.recv(frow(-3), fz[3], zs[7])
    wire.recv(frow(3), fz[5], zs[1])
    wire.recv(frow(4), fz[4], zs[6])
    for j in (0, 1, 3, 2):
        take(j)
    if upto < 1:
        for load in loads + [load_down]:
            load.wait()
        out[...] = X[my_rows, :]
        return finish()

    flags = F[...].reshape(32, 128)
    lanes = jnp.dot(flags.astype(BF), SPR[...], preferred_element_type=F32)
    owner = lax.broadcasted_iota(jnp.int32, (32, 512), 1) // 16
    unit = lax.broadcasted_iota(jnp.int32, (32, 512), 0)
    active = jnp.sum(jnp.where(unit == owner, lanes, 0.0), axis=0, keepdims=True)
    upto_here = jnp.dot(jnp.broadcast_to(active, (16, 512)).astype(BF), TRI[...], preferred_element_type=F32)[0:1, :]
    want = lax.broadcasted_iota(jnp.int32, (64, 512), 0).astype(F32)
    goal = jnp.where(active > 0.5, upto_here - 1.0, -1.0)
    choose = jnp.where(goal == want, 1.0, 0.0).astype(BF)
    g = GN[...]
    XF[...] = jnp.dot(choose, X[...], preferred_element_type=F32)
    NG = len(GROUPS)

    def cols(p):
        lo, w = GROUPS[p]
        return slice(2 * lo, 2 * lo + 2 * w)

    def sq_rounds(ss, rr):
        slots = [wire.slot() for _ in range(8)]
        wire.send(ss, rr.at[0], slots[0], core)
        yield
        wire.recv(rr.at[0], slots[0], core)
        rr[8] = ss[...] + rr[0]
        for q in range(7):
            wire.send(rr.at[8], rr.at[q + 1], slots[q + 1], xys[q])
        yield
        total = rr[8]
        for q in range(7):
            wire.recv(rr.at[q + 1], slots[q + 1], sec(dx=-around[q][0], dy=around[q][1]))
            total = total + rr[q + 1]
        rr[9] = total
        yield

    def scale_of(rr, first, count):
        line = rr[9, pl.ds(first // 128, 1), :]
        picked = jnp.where(eye(count, 128, first % 128), line, 0.0)
        return lax.rsqrt(jnp.sum(picked, axis=1, keepdims=True) / FEATURES + EPS)

    def act(gate, up):
        return (gate / (1.0 + jnp.exp(-gate)) * up).astype(BF)

    def packed(n):
        v = XF[...]
        C[n] = (v * g).astype(BF)
        col = jnp.sum(v * v, axis=1, keepdims=True)
        s2 = S2.at[n]
        s2[...] = jnp.zeros((8, 128), F32)
        s2[0:1, :] = jnp.sum(jnp.where(eye(64, 128), col, 0.0), axis=0, keepdims=True)
        g2, h2all = G2.at[n], H2.at[n]
        for p in range(NG):
            if n == 0:
                loads[2 * p].wait()
                loads[2 * p + 1].wait()
            lo, w = GROUPS[p]
            prod = jnp.dot(C[n], W[:, cols(p)], preferred_element_type=F32).astype(BF)
            g2[:, 512 * p:512 * p + w] = prod[:, 0:w]
            g2[:, 512 * p + 256:512 * p + 256 + w] = prod[:, w:2 * w]
            if w < 256:
                g2[:, 512 * p + w:512 * p + 256] = jnp.zeros((64, 256 - w), BF)
                g2[:, 512 * p + 256 + w:512 * p + 512] = jnp.zeros((64, 256 - w), BF)
        slot = wire.slot()
        wire.send(g2.at[pl.ds(mo((1 - c) * 32, 32), 32), :], c2r.at[n], slot, core)
        sq = sq_rounds(s2, S2r.at[n])
        next(sq)
        yield
        core_rows = pl.ds(mo(c * 32, 32), 32)
        wire.recv(c2r.at[n], slot, core)
        g2[core_rows, :] = (g2[core_rows, :].astype(F32) + c2r[n].astype(F32)).astype(BF)

        def block(dx, dy):
            return g2.at[pl.ds(mo(c * 32 + ((yl + dy) % 2) * 16, 16), 16), pl.ds(mo(((x + dx) % 4) * 512, 512), 512)]
        slots = [wire.slot() for _ in range(7)]
        for q, (dx, dy) in enumerate(around):
            wire.send(block(dx, dy), x2r.at[n, q], slots[q], xys[q])
        next(sq)
        yield
        total = block(0, 0)[...].astype(F32)
        for q, (dx, dy) in enumerate(around):
            wire.recv(x2r.at[n, q], slots[q], sec(dx=-dx, dy=dy))
            total = total + x2r[n, q].astype(F32)
        next(sq)
        total = total * scale_of(S2r.at[n], c * 32 + yl * 16, 16)

        def hid(dx, dy):
            return h2all.at[pl.ds(mo(c * 32 + ((yl + dy) % 2) * 16, 16), 16), pl.ds(mo(((x + dx + 4) % 4) * 256, 256), 256)]
        hid(0, 0)[...] = act(total[:, 0:256], total[:, 256:512])
        slots = [wire.slot() for _ in range(7)]
        for q in range(7):
            same(hid(0, 0), slots[q], xys[q])
        yield
        for q, (dx, dy) in enumerate(around):
            wire.recv(hid(-dx, dy), slots[q], sec(dx=-dx, dy=dy))
        slot = wire.slot()
        same(h2all.at[core_rows, :], slot, core)
        yield
        wire.recv(h2all.at[pl.ds(mo((1 - c) * 32, 32), 32), :], slot, core)
        yield

    def all_sum(prod):
        folded = jnp.concatenate([prod[:, 0:256].reshape(8, 8, 256), prod[:, 256:512].reshape(8, 8, 256)], axis=1)
        PF[...] = folded.reshape(128, 256).astype(BF)

        def blk16(ref, dz):
            return ref.at[pl.ds(mo(((z + dz + 8) % 8) * 16, 16), 16), :]
        slots = {d: wire.slot() for d in range(1, 8)}
        for d in (4, 3, 5, 2, 6, 1, 7):
            wire.send(blk16(PF, d), zr.at[d - 1], slots[d], zs[d])
        yield
        total = blk16(PF, 0)[...].astype(F32)
        for d in (1, 7, 2, 6, 3, 5, 4):
            wire.recv(zr.at[d - 1], slots[d], zs[8 - d])
            total = total + zr[d - 1].astype(F32)
        yex[...] = total.astype(BF)
        ys = {j: wire.slot() for j in (1, 2, 3)}
        for j in (2, 1, 3):
            wire.send(yex, z3.at[j - 1], ys[j], yhs[j])
        yield
        for j in (1, 3, 2):
            wire.recv(z3.at[j - 1], ys[j], yhs[4 - j])
            total = total + z3[j - 1].astype(F32)
        blk16(ZA, 0)[...] = total.astype(BF)
        zg = {d: wire.slot() for d in range(1, 8)}
        for d in (4, 3, 5, 2, 6, 1, 7):
            same(blk16(ZA, 0), zg[d], zs[d])
        yield
        for d in (1, 7, 2, 6, 3, 5, 4):
            wire.recv(blk16(ZA, -d), zg[d], zs[8 - d])
        got = ZA[...].astype(F32).reshape(8, 16, 256)
        change = jnp.concatenate([got[:, 0:8, :].reshape(64, 256), got[:, 8:16, :].reshape(64, 256)], axis=1)
        XF[...] = XF[...] + change
        yield

    def ring_reduce(src, ub, db, ts, tb, ybuf, result, block_done):
        def part(off, h):
            return src.at[pl.ds(mo(((z + off + 8) % 8) * 64 + h * 32, 32), 32), :]

        us = {(k, h): wire.slot() for k in range(4) for h in range(2)}
        ds = {(k, h): wire.slot() for k in range(4) for h in range(2)}
        block_done(4)
        wire.send(part(4, 0), ub.at[0, 0:32, :], us[0, 0], ups)
        wire.send(part(4, 1), db.at[0, 32:64, :], ds[0, 1], downs)
        for k in (1, 2, 3):
            block_done(4 - k)
            yield
            for h in ((1, 0) if k == 1 else (0, 1)):
                hu, hd = h, 1 - h
                if k > 1 or hu == 0:
                    got = ub.at[k - 1, hu * 32:hu * 32 + 32, :]
                    wire.recv(got, us[k - 1, hu], downs)
                    acc = part(4 - k, hu)
                    acc[...] = (acc[...].astype(F32) + got[...].astype(F32)).astype(BF)
                wire.send(part(4 - k, hu), ub.at[k, hu * 32:hu * 32 + 32, :], us[k, hu], ups)
                if k > 1 or hd == 1:
                    got = db.at[k - 1, hd * 32:hd * 32 + 32, :]
                    wire.recv(got, ds[k - 1, hd], ups)
                    acc = part(k - 4, hd)
                    acc[...] = (acc[...].astype(F32) + got[...].astype(F32)).astype(BF)
                wire.send(part(k - 4, hd), db.at[k, hd * 32:hd * 32 + 32, :], ds[k, hd], downs)
        yield
        for h in (0, 1):
            a, b = ub.at[3, h * 32:h * 32 + 32, :], db.at[3, h * 32:h * 32 + 32, :]
            wire.recv(a, us[3, h], downs)
            wire.recv(b, ds[3, h], ups)
            total = part(0, h)[...].astype(F32) + a[...].astype(F32) + b[...].astype(F32)
            ts[h * 32:h * 32 + 32, :] = total
            tb[h * 32:h * 32 + 32, :] = total.astype(BF)
        ys = {j: wire.slot() for j in (1, 2, 3)}
        for j in (2, 1, 3):
            wire.send(tb.at[pl.ds(mo(((yh + j) % 4) * 16, 16), 16), :], ybuf.at[j - 1], ys[j], yhs[j])
        yield
        total = ts[pl.ds(mo(yh * 16, 16), 16), :]
        for j in (1, 3, 2):
            wire.recv(ybuf.at[j - 1], ys[j], yhs[4 - j])
            total = total + ybuf[j - 1].astype(F32)
        result.append(total)
        yield

    def bulk():
        for b in range(4):
            part_cols = []
            for q in range(4):
                lo = b * 128 + q * 32
                v = X[lo:lo + 32, :].astype(F32)
                XG[lo:lo + 32, :] = (v * g).astype(BF)
                part_cols.append(jnp.sum(v * v, axis=1, keepdims=True))
            col = jnp.concatenate(part_cols, axis=0)
            SS[b:b + 1, :] = jnp.sum(jnp.where(eye(128, 128), col, 0.0), axis=0, keepdims=True)
        SS[4:8, :] = jnp.zeros((4, 128), F32)

        def gate_up(row0, p, dst):
            @pl.loop(0, 2)
            def _(i):
                r = mo(i * 128, 128)
                dst[pl.ds(r, 128), cols(p)] = jnp.dot(
                    XG[pl.ds(mo(row0 + r, 128), 128), :], W[:, cols(p)],
                    preferred_element_type=F32).astype(BF)

        cslot = [wire.slot() for _ in range(NG)]
        for p in range(NG):
            gate_up((1 - c) * 256, p, snd)
            wire.send(snd.at[:, cols(p)], crecv.at[:, cols(p)], cslot[p], core)
        sq = sq_rounds(SS, SSr)
        next(sq)
        yield
        for p in range(NG):
            gate_up(c * 256, p, own)
        yield

        def blk(off, h):
            return pl.ds(mo(((x + off) % 4) * 64 + h * 32, 32), 32)

        xslot = [[wire.slot() for _ in range(6)] for _ in range(NG)]
        for p in range(NG):
            wire.recv(crecv.at[:, cols(p)], cslot[p], core)

            @pl.loop(0, 8)
            def _(i):
                r = pl.ds(mo(i * 32, 32), 32)
                own[r, cols(p)] = (own[r, cols(p)].astype(F32) + crecv[r, cols(p)].astype(F32)).astype(BF)
            wire.send(own.at[blk(2, 0), cols(p)], fwdp.at[:, cols(p)], xslot[p][0], xs[1])
            wire.send(own.at[blk(2, 1), cols(p)], fwdm.at[:, cols(p)], xslot[p][1], xs[3])
            wire.send(own.at[blk(1, 1), cols(p)], dirp.at[32:64, cols(p)], xslot[p][2], xs[1])
            wire.send(own.at[blk(3, 0), cols(p)], dirm.at[0:32, cols(p)], xslot[p][3], xs[3])
        next(sq)
        yield
        for p in range(NG):
            wire.recv(fwdp.at[:, cols(p)], xslot[p][0], xs[3])
            r = blk(1, 0)
            own[r, cols(p)] = (own[r, cols(p)].astype(F32) + fwdp[:, cols(p)].astype(F32)).astype(BF)
            wire.send(own.at[r, cols(p)], dirp.at[0:32, cols(p)], xslot[p][4], xs[1])
            wire.recv(fwdm.at[:, cols(p)], xslot[p][1], xs[1])
            r = blk(3, 1)
            own[r, cols(p)] = (own[r, cols(p)].astype(F32) + fwdm[:, cols(p)].astype(F32)).astype(BF)
            wire.send(own.at[r, cols(p)], dirm.at[32:64, cols(p)], xslot[p][5], xs[3])
        next(sq)
        yield
        yslot = [wire.slot() for _ in range(NG)]
        for p in range(NG):
            wire.recv(dirp.at[32:64, cols(p)], xslot[p][2], xs[3])
            wire.recv(dirm.at[0:32, cols(p)], xslot[p][3], xs[1])
            wire.recv(dirp.at[0:32, cols(p)], xslot[p][4], xs[3])
            wire.recv(dirm.at[32:64, cols(p)], xslot[p][5], xs[1])

            def xsum(h):
                hr = pl.ds(mo(h * 32, 32), 32)
                return (own[blk(0, h), cols(p)].astype(F32) + dirp[hr, cols(p)].astype(F32)
                        + dirm[hr, cols(p)].astype(F32))
            ysnd[:, cols(p)] = xsum(other).astype(BF)
            wire.send(ysnd.at[:, cols(p)], yrecv.at[:, cols(p)], yslot[p], ydev)
            tot[:, cols(p)] = xsum(mine)
        yield
        scale = scale_of(SSr, c * 256 + x * 64 + yl * 32, 32)

        def hrows(off, h):
            return pl.ds(mo(c * 256 + ((x + off) % 4) * 64 + h * 32, 32), 32)

        hy = [wire.slot() for _ in range(NG)]
        hx = [[wire.slot() for _ in range(6)] for _ in range(NG)]
        hc = [wire.slot() for _ in range(NG)]

        def hcols(p):
            lo, w = GROUPS[p]
            return slice(lo, lo + w)

        def hsend(off, h, p, slot, dev):
            same(H.at[hrows(off, h), hcols(p)], slot, dev)

        def hrecv(off, h, p, slot, dev):
            wire.recv(H.at[hrows(off, h), hcols(p)], slot, dev)

        for p in range(NG):
            lo, w = GROUPS[p]
            wire.recv(yrecv.at[:, cols(p)], yslot[p], ydev)
            gate = (tot[:, 2 * lo:2 * lo + w] + yrecv[:, 2 * lo:2 * lo + w].astype(F32)) * scale
            up = (tot[:, 2 * lo + w:2 * lo + 2 * w] + yrecv[:, 2 * lo + w:2 * lo + 2 * w].astype(F32)) * scale
            H[hrows(0, mine), hcols(p)] = act(gate, up)
            hsend(0, mine, p, hy[p], ydev)
            hsend(0, mine, p, hx[p][0], xs[1])
            hsend(0, mine, p, hx[p][1], xs[3])
        yield
        for p in range(NG):
            hrecv(0, other, p, hy[p], ydev)
            hsend(0, other, p, hx[p][2], xs[1])
            hsend(0, other, p, hx[p][3], xs[3])
            hrecv(3, mine, p, hx[p][0], xs[3])
            hsend(3, mine, p, hx[p][4], xs[1])
            hrecv(1, mine, p, hx[p][1], xs[1])
        yield
        for p in range(NG):
            hrecv(3, other, p, hx[p][2], xs[3])
            hrecv(1, other, p, hx[p][3], xs[1])
            hsend(1, other, p, hx[p][5], xs[3])
        yield
        for p in range(NG):
            hrecv(2, mine, p, hx[p][4], xs[3])
            hrecv(2, other, p, hx[p][5], xs[1])
            half = H.at[pl.ds(mo(c * 256, 256), 256), hcols(p)]
            same(half, hc[p], core)
        yield
        for p in range(NG):
            wire.recv(H.at[pl.ds(mo((1 - c) * 256, 256), 256), hcols(p)], hc[p], core)

        def down_pair(off):
            a = pl.ds(mo(((z + off) % 8) * 64, 64), 64)
            b = pl.ds(mo(((z - off + 8) % 8) * 64, 64), 64)
            if off == 4:
                b = pl.ds(mo(z * 64, 64), 64)
            both = jnp.concatenate([H[a, :], H[b, :]], axis=0)
            prod = jnp.dot(both, WD[...], preferred_element_type=F32).astype(BF)
            D[a, :] = prod[0:64]
            D[b, :] = prod[64:128]

        delta = []
        for _ in ring_reduce(D, upb, dnb, tsum, tbf, yb, delta, down_pair):
            if not delta:
                yield
        st[...] = tok_rows() + delta[0]
        yield

    def tok_rows():
        return X[my_rows, :].astype(F32)

    def down_of(n):
        return jnp.dot(H2[n, :, 0:896], WD[...], preferred_element_type=F32)

    def run(*gens):
        for gen in gens:
            next(gen)

    p1, big = packed(0), bulk()

    def stop(*gens):
        for gen in gens:
            for _ in gen:
                pass
        load_down.wait()
        out[...] = XF[0:16, :].astype(BF)
        finish()

    run(p1)
    run(p1, big)
    run(big)
    run(p1)
    run(p1)
    run(p1)
    load_down.wait()
    if upto < 2:
        return stop(big)
    total = all_sum(down_of(0))
    run(total)
    run(big)
    run(total)
    run(big)
    run(total)
    run(big)
    run(total)
    if upto < 3:
        return stop(big)
    p2 = packed(1)
    run(p2)
    run(big)
    run(p2)
    run(big)
    run(p2)
    run(big)
    run(p2)
    run(big, p2)
    run(big)

    down2 = down_of(1).astype(BF)
    counts = jnp.sum(flags, axis=1, keepdims=True)
    before = jnp.sum(jnp.where(unit < owner, counts, 0.0), axis=0, keepdims=True)
    here = jnp.sum(jnp.where(unit == owner, counts, 0.0), axis=0, keepdims=True)
    slot_lane = lax.broadcasted_iota(jnp.int32, (1, 512), 1) % 16
    place = (slot_lane % 8).astype(F32)
    goal = jnp.where(place < here, before + place, -1.0)
    hit = jnp.where(goal == want, 1.0, 0.0)
    left = jnp.where(slot_lane < 8, hit, 0.0).astype(BF)
    right = jnp.where(slot_lane >= 8, hit, 0.0).astype(BF)
    dims = (((0,), (0,)), ((), ()))
    D2[...] = (lax.dot_general(left, down2[:, 0:256], dims, preferred_element_type=F32)
               + lax.dot_general(right, down2[:, 256:512], dims, preferred_element_type=F32)).astype(BF)
    back = []
    last = ring_reduce(D2, upb2, dnb2, tsum2, tbf2, yb2, back, lambda off: None)

    for k in range(6):
        run(last)
        if k < 5:
            for _ in range(1 if k else 2):
                if next(big, done) is done:
                    break
    for _ in big:
        pass
    back = back[0]
    act_row = (RV[...] == 2).astype(F32)
    sub = lax.broadcasted_iota(jnp.int32, (16, 16), 0)
    lane = lax.broadcasted_iota(jnp.int32, (16, 16), 1)
    act_col = jnp.sum(jnp.where(sub == lane, act_row, 0.0), axis=1, keepdims=True)
    place_col = jnp.sum(jnp.where(lane <= sub, act_row, 0.0), axis=1, keepdims=True) - 1.0
    acc_l = jnp.zeros((16, 256), F32)
    acc_r = jnp.zeros((16, 256), F32)
    for k in range(8):
        put = jnp.where((place_col == k) & (act_col > 0.5), 1.0, 0.0)
        acc_l = acc_l + put * back[k:k + 1, :]
        acc_r = acc_r + put * back[k + 8:k + 9, :]
    out[...] = (st[...] + jnp.concatenate([acc_l, acc_r], axis=1)).astype(BF)
    finish()


def body(upto, tokens, norm_gain, gate_weight, up_weight, down_weight, revisit):
    vm = lambda *shape: pltpu.VMEM(shape, BF)
    vf = lambda *shape: pltpu.VMEM(shape, F32)
    vspec, hbm = pl.BlockSpec(memory_space=pltpu.VMEM), pl.BlockSpec(memory_space=pltpu.MemorySpace.HBM)
    scratch = [
        vm(512, 512), vm(512, 512), vm(512, 1792), vm(896, 512), vf(32, 1, 128), vf(1, 512),
        pltpu.VMEM((1, 16), jnp.int32),
        vm(256, 1792), vm(256, 1792), vm(256, 1792), vm(32, 1792), vm(32, 1792), vm(64, 1792), vm(64, 1792),
        vm(32, 1792), vm(32, 1792), vf(32, 1792), vm(512, 896),
        vm(512, 512), vm(4, 64, 512), vm(4, 64, 512), vf(64, 512), vm(64, 512), vm(3, 16, 512),
        vf(8, 128), vf(10, 8, 128), vf(2, 8, 128), vf(2, 10, 8, 128), vm(512, 512), vm(128, 512),
        vf(64, 512), vm(2, 64, 512), vm(2, 64, 2048), vm(2, 32, 2048), vm(2, 7, 16, 512), vm(2, 64, 1024),
        vm(128, 256), vm(7, 16, 256), vm(3, 16, 256), vm(16, 256), vm(128, 256),
        vm(512, 256), vm(4, 64, 256), vm(4, 64, 256), vf(64, 256), vm(64, 256), vm(3, 16, 256),
        vf(16, 512),
        pltpu.SemaphoreType.DMA((12,)), pltpu.SemaphoreType.DMA((320,)), pltpu.SemaphoreType.DMA((320,)),
    ]
    return pl.pallas_call(
        functools.partial(kernel, upto),
        out_shape=jax.ShapeDtypeStruct((16, 512), BF),
        in_specs=[hbm] * 6,
        out_specs=vspec,
        scratch_shapes=scratch,
        compiler_params=pltpu.CompilerParams(
            collective_id=0, has_side_effects=True, vmem_limit_bytes=40 * 1024 * 1024),
        cost_estimate=pl.CostEstimate(flops=2000000000, bytes_accessed=3000000, transcendentals=30000),
        name="two_pass_block",
    )(tokens, norm_gain.reshape(1, 512), revisit.reshape(1, 16), gate_weight, up_weight, down_weight)


def solution(mesh, upto=LAST):
    placed = (P("tp", "section"), P("section"), P("section", "tp"), P("section", "tp"), P("tp", "section"), P("tp"))
    return jax.shard_map(functools.partial(body, upto), mesh=mesh, in_specs=placed,
                         out_specs=P("tp", "section"), check_vma=False)
```

```python
import functools
import jax
import jax.numpy as jnp
from jax import lax
from jax.experimental import pallas as pl
from jax.experimental.pallas import tpu as pltpu
from jax.sharding import PartitionSpec as P

BF, F32 = jnp.bfloat16, jnp.float32
GROUPS = ((0, 256), (256, 256), (512, 256), (768, 128))
FEATURES = 8192.0
EPS = 1e-5
LAST = 99


def mo(value, unit):
    return pl.multiple_of(value, unit)


def eye(rows, lanes, offset=0):
    row = lax.broadcasted_iota(jnp.int32, (rows, lanes), 0)
    lane = lax.broadcasted_iota(jnp.int32, (rows, lanes), 1)
    return lane == row + offset


class Wire:
    def __init__(self, send_sem, recv_sem):
        self.send_sem, self.recv_sem = send_sem, recv_sem
        self.count, self.sent = 0, []

    def slot(self):
        self.count += 1
        return self.count - 1

    def send(self, src, dst, slot, dev):
        copy = pltpu.make_async_remote_copy(
            src_ref=src, dst_ref=dst, send_sem=self.send_sem.at[slot], recv_sem=self.recv_sem.at[slot],
            device_id=dev, device_id_type=pl.DeviceIdType.MESH)
        copy.start()
        self.sent.append(copy)

    def recv(self, dst, slot, dev):
        pltpu.make_async_remote_copy(
            src_ref=dst, dst_ref=dst, send_sem=self.send_sem.at[slot], recv_sem=self.recv_sem.at[slot],
            device_id=dev, device_id_type=pl.DeviceIdType.MESH).wait_recv()

    def drain(self):
        for copy in self.sent:
            copy.wait_send()


def kernel(upto, tok, gain, rev, wg, wu, wd, out,
           X, W, WD, F, GN, RV, G, own, crecv, fwdp, fwdm, dirp, dirm, ysnd, yrecv, tot, H,
           D, q4, q3, n1, n2, tsum, tbf, yb, SS, SSr, S2, S2r, TRI, SPR,
           XF, C, G2, c2r, x2r, H2, PF, zr, z3, yex, ZA, st,
           wsem, send_sem, recv_sem):
    s, t = lax.axis_index("section"), lax.axis_index("tp")
    c, x, yl = s % 2, (s // 2) % 4, s // 8
    z, yh = t // 4, t % 4
    wire = Wire(send_sem, recv_sem)
    mine, other = yl, 1 - yl

    def sec(dc=0, dx=0, dy=0):
        return ((((yl + dy + 2) % 2) * 4 + (x + dx + 4) % 4) * 2 + (c + dc) % 2, t)

    def tpd(dz=0, dh=0):
        return (s, ((z + dz + 8) % 8) * 4 + (yh + dh + 4) % 4)

    core, ydev = sec(dc=1), sec(dy=1)
    xs = {j: sec(dx=j) for j in (1, 2, 3)}
    zs = {j: tpd(dz=j) for j in range(1, 8)}
    ups, downs = zs[1], zs[7]
    yhs = {j: tpd(dh=j) for j in (1, 2, 3)}
    around = [(2, 1), (2, 0), (1, 1), (3, 1), (1, 0), (3, 0), (0, 1)]
    xys = [sec(dx=a, dy=b) for a, b in around]

    loads = []
    for g, (lo, w) in enumerate(GROUPS):
        loads.append(pltpu.make_async_copy(wg.at[:, lo:lo + w], W.at[:, 2 * lo:2 * lo + w], wsem.at[2 * g]))
        loads.append(pltpu.make_async_copy(wu.at[:, lo:lo + w], W.at[:, 2 * lo + w:2 * lo + 2 * w], wsem.at[2 * g + 1]))
    load_down = pltpu.make_async_copy(wd, WD, wsem.at[8])
    my_rows = pl.ds(mo(t * 16, 16), 16)
    small = [pltpu.make_async_copy(tok, X.at[my_rows, :], wsem.at[9]), pltpu.make_async_copy(rev, RV, wsem.at[10]),
             pltpu.make_async_copy(gain, GN, wsem.at[11])]
    for load in small + loads + [load_down]:
        load.start()

    barrier = pltpu.get_barrier_semaphore()
    peers = [core] + list(zs.values()) + list(yhs.values()) + xys
    for peer in peers:
        pl.semaphore_signal(barrier, inc=1, device_id=peer, device_id_type=pl.DeviceIdType.MESH)
    TRI[...] = jnp.where(lax.broadcasted_iota(jnp.int32, (512, 512), 0)
                         <= lax.broadcasted_iota(jnp.int32, (512, 512), 1), 1.0, 0.0).astype(BF)
    SPR[...] = jnp.where(lax.broadcasted_iota(jnp.int32, (128, 512), 1) % 16
                         == lax.broadcasted_iota(jnp.int32, (128, 512), 0), 1.0, 0.0).astype(BF)
    for load in small:
        load.wait()
    flag_row = jnp.where(RV[...] == 2, 1.0, 0.0)
    F[t] = jnp.concatenate([flag_row, jnp.zeros((1, 112), F32)], axis=1)
    pl.semaphore_wait(barrier, len(peers))
    done = object()

    def finish():
        wire.drain()

    def rows(dz, j):
        return X.at[pl.ds(mo(((z + dz + 8) % 8) * 64 + ((yh - j + 4) % 4) * 16, 16), 16), :]

    def frow(dz):
        return F.at[pl.ds(((z + dz + 8) % 8) * 4, 4)]

    def same(ref, slot, dev):
        wire.send(ref, ref, slot, dev)

    fy = {j: wire.slot() for j in (1, 2, 3)}
    fz = {d: wire.slot() for d in range(1, 8)}
    sy = {j: wire.slot() for j in (1, 2, 3)}
    sz = {(d, j): wire.slot() for d in range(1, 8) for j in range(4)}
    for j in (2, 1, 3):
        same(F.at[pl.ds(t, 1)], fy[j], yhs[j])
        same(rows(0, 0), sy[j], yhs[j])

    def spread(j):
        for d in (2, 6, 1, 7):
            same(rows(0, j), sz[d, j], zs[d])

    def relay(j):
        wire.recv(rows(-2, j), sz[2, j], zs[6])
        if j in (0, 1):
            same(rows(-2, j), sz[4, j], zs[2])
        same(rows(-2, j), sz[3, j], zs[1])
        wire.recv(rows(2, j), sz[6, j], zs[2])
        if j in (2, 3):
            same(rows(2, j), sz[4, j], zs[6])
        same(rows(2, j), sz[5, j], zs[7])

    def take(d):
        for j in (0, 1, 3, 2):
            if d == 4:
                wire.recv(rows(4, j), sz[4, j], zs[6] if j in (0, 1) else zs[2])
            else:
                wire.recv(rows(-d, j), sz[d, j], zs[7])
                wire.recv(rows(d, j), sz[8 - d, j], zs[1])

    NG = len(GROUPS)

    def cols(p):
        lo, w = GROUPS[p]
        return slice(2 * lo, 2 * lo + 2 * w)

    cslot = {d: wire.slot() for d in range(8)}
    g = GN[...]

    def half_rows(d, cc):
        return pl.ds(mo(((z + d) % 8) * 64 + cc * 32, 32), 32)

    def unit_rows(d):
        return pl.ds(mo(((z + d) % 8) * 32, 32), 32)

    def gate_up(ds):
        blocks = [pl.ds(mo(((z + d) % 8) * 64, 64), 64) for d in ds]
        v = jnp.concatenate([X[b, :] for b in blocks], axis=0).astype(F32)
        scaled = (v * g).astype(BF)
        col = jnp.sum(v * v, axis=1, keepdims=True)
        for n, d in enumerate(ds):
            SS[pl.ds((z + d) % 8, 1), :] = jnp.sum(
                jnp.where(eye(64, 128), col[n * 64:n * 64 + 64], 0.0), axis=0, keepdims=True)
        for p in range(NG):
            prod = jnp.dot(scaled, W[:, cols(p)], preferred_element_type=F32).astype(BF)
            for n, b in enumerate(blocks):
                G[b, cols(p)] = prod[n * 64:n * 64 + 64]
        for d in ds:
            wire.send(G.at[half_rows(d, 1 - c), :], crecv.at[unit_rows(d), :], cslot[d], core)

    spread(0)
    for j in (1, 3):
        wire.recv(rows(0, j), sy[j], yhs[4 - j])
        spread(j)
    relay(0)
    for j in (1, 2, 3):
        wire.recv(F.at[pl.ds(z * 4 + (yh - j + 4) % 4, 1)], fy[j], yhs[4 - j])
    for d in (2, 6, 1, 7):
        same(frow(0), fz[d], zs[d])
    wire.recv(rows(0, 2), sy[2], yhs[2])
    spread(2)
    relay(1)
    relay(3)
    for load in loads:
        load.wait()
    if upto not in (0, 7, 70, 71, 72):
        gate_up((0,))
    wire.recv(frow(-2), fz[2], zs[6])
    same(frow(-2), fz[4], zs[2])
    same(frow(-2), fz[3], zs[1])
    wire.recv(frow(2), fz[6], zs[2])
    same(frow(2), fz[5], zs[7])
    relay(2)
    take(1)
    if upto not in (0, 7, 70, 71, 72):
        gate_up((1, 7))
        gate_up((2, 6))
    wire.recv(frow(-1), fz[1], zs[7])
    wire.recv(frow(1), fz[7], zs[1])
    wire.recv(frow(-3), fz[3], zs[7])
    wire.recv(frow(3), fz[5], zs[1])
    wire.recv(frow(4), fz[4], zs[6])
    take(3)
    take(4)
    if upto < 1:
        load_down.wait()
        out[...] = X[my_rows, :]
        return finish()

    flags = F[...].reshape(32, 128)
    lanes = jnp.dot(flags.astype(BF), SPR[...], preferred_element_type=F32)
    owner = lax.broadcasted_iota(jnp.int32, (32, 512), 1) // 16
    unit = lax.broadcasted_iota(jnp.int32, (32, 512), 0)
    active = jnp.sum(jnp.where(unit == owner, lanes, 0.0), axis=0, keepdims=True)
    upto_here = jnp.dot(jnp.broadcast_to(active, (16, 512)).astype(BF), TRI[...], preferred_element_type=F32)[0:1, :]
    want = lax.broadcasted_iota(jnp.int32, (64, 512), 0).astype(F32)
    goal = jnp.where(active > 0.5, upto_here - 1.0, -1.0)
    choose = jnp.where(goal == want, 1.0, 0.0).astype(BF)
    XF[...] = jnp.dot(choose, X[...], preferred_element_type=F32)

    def sq_rounds(ss, rr):
        slots = [wire.slot() for _ in range(8)]
        wire.send(ss, rr.at[0], slots[0], core)
        yield
        wire.recv(rr.at[0], slots[0], core)
        rr[8] = ss[...] + rr[0]
        for q in range(7):
            wire.send(rr.at[8], rr.at[q + 1], slots[q + 1], xys[q])
        yield
        total = rr[8]
        for q in range(7):
            wire.recv(rr.at[q + 1], slots[q + 1], sec(dx=-around[q][0], dy=around[q][1]))
            total = total + rr[q + 1]
        rr[9] = total
        yield

    def scale_of(rr, first, count):
        line = rr[9, pl.ds(first // 128, 1), :]
        picked = jnp.where(eye(count, 128, first % 128), line, 0.0)
        return lax.rsqrt(jnp.sum(picked, axis=1, keepdims=True) / FEATURES + EPS)

    def act(gate, up):
        return (gate / (1.0 + jnp.exp(-gate)) * up).astype(BF)

    def packed(n):
        v = XF[...]
        C[n] = (v * g).astype(BF)
        col = jnp.sum(v * v, axis=1, keepdims=True)
        s2 = S2.at[n]
        s2[...] = jnp.zeros((8, 128), F32)
        s2[0:1, :] = jnp.sum(jnp.where(eye(64, 128), col, 0.0), axis=0, keepdims=True)
        g2, h2all = G2.at[n], H2.at[n]
        for p in range(NG):
            lo, w = GROUPS[p]
            prod = jnp.dot(C[n], W[:, cols(p)], preferred_element_type=F32).astype(BF)
            g2[:, 512 * p:512 * p + w] = prod[:, 0:w]
            g2[:, 512 * p + 256:512 * p + 256 + w] = prod[:, w:2 * w]
            if w < 256:
                g2[:, 512 * p + w:512 * p + 256] = jnp.zeros((64, 256 - w), BF)
                g2[:, 512 * p + 256 + w:512 * p + 512] = jnp.zeros((64, 256 - w), BF)
        slot = wire.slot()
        wire.send(g2.at[pl.ds(mo((1 - c) * 32, 32), 32), :], c2r.at[n], slot, core)
        sq = sq_rounds(s2, S2r.at[n])
        next(sq)
        yield
        core_rows = pl.ds(mo(c * 32, 32), 32)
        wire.recv(c2r.at[n], slot, core)
        g2[core_rows, :] = (g2[core_rows, :].astype(F32) + c2r[n].astype(F32)).astype(BF)

        def block(dx, dy):
            return g2.at[pl.ds(mo(c * 32 + ((yl + dy) % 2) * 16, 16), 16), pl.ds(mo(((x + dx) % 4) * 512, 512), 512)]
        slots = [wire.slot() for _ in range(7)]
        for q, (dx, dy) in enumerate(around):
            wire.send(block(dx, dy), x2r.at[n, q], slots[q], xys[q])
        next(sq)
        yield
        total = block(0, 0)[...].astype(F32)
        for q, (dx, dy) in enumerate(around):
            wire.recv(x2r.at[n, q], slots[q], sec(dx=-dx, dy=dy))
            total = total + x2r[n, q].astype(F32)
        next(sq)
        total = total * scale_of(S2r.at[n], c * 32 + yl * 16, 16)

        def hid(dx, dy):
            return h2all.at[pl.ds(mo(c * 32 + ((yl + dy) % 2) * 16, 16), 16), pl.ds(mo(((x + dx + 4) % 4) * 256, 256), 256)]
        hid(0, 0)[...] = act(total[:, 0:256], total[:, 256:512])
        slots = [wire.slot() for _ in range(7)]
        for q in range(7):
            same(hid(0, 0), slots[q], xys[q])
        yield
        for q, (dx, dy) in enumerate(around):
            wire.recv(hid(-dx, dy), slots[q], sec(dx=-dx, dy=dy))
        slot = wire.slot()
        same(h2all.at[core_rows, :], slot, core)
        yield
        wire.recv(h2all.at[pl.ds(mo((1 - c) * 32, 32), 32), :], slot, core)
        yield

    def all_sum(n, prod, result):
        folded = jnp.concatenate([prod[:, 0:256].reshape(8, 8, 256), prod[:, 256:512].reshape(8, 8, 256)], axis=1)
        pf, za = PF.at[n], ZA.at[n]
        pf[...] = folded.reshape(128, 256).astype(BF)

        def blk16(ref, dz):
            return ref.at[pl.ds(mo(((z + dz + 8) % 8) * 16, 16), 16), :]
        slots = {d: wire.slot() for d in range(1, 8)}
        for d in (4, 3, 5, 2, 6, 1, 7):
            wire.send(blk16(pf, d), zr.at[n, d - 1], slots[d], zs[d])
        yield
        total = blk16(pf, 0)[...].astype(F32)
        for d in (1, 7, 2, 6, 3, 5, 4):
            wire.recv(zr.at[n, d - 1], slots[d], zs[8 - d])
            total = total + zr[n, d - 1].astype(F32)
        yex[n] = total.astype(BF)
        ys = {j: wire.slot() for j in (1, 2, 3)}
        for j in (2, 1, 3):
            wire.send(yex.at[n], z3.at[n, j - 1], ys[j], yhs[j])
        yield
        total = yex[n].astype(F32)
        for j in (1, 3, 2):
            wire.recv(z3.at[n, j - 1], ys[j], yhs[4 - j])
            total = total + z3[n, j - 1].astype(F32)
        blk16(za, 0)[...] = total.astype(BF)
        zg = {d: wire.slot() for d in range(1, 8)}
        for d in (4, 3, 5, 2, 6, 1, 7):
            same(blk16(za, 0), zg[d], zs[d])
        yield
        for d in (1, 7, 2, 6, 3, 5, 4):
            wire.recv(blk16(za, -d), zg[d], zs[8 - d])
        got = za[...].astype(F32).reshape(8, 16, 256)
        result.append(jnp.concatenate(
            [got[:, 0:8, :].reshape(64, 256), got[:, 8:16, :].reshape(64, 256)], axis=1))
        yield

    def z_reduce(result, blocks):
        def part(off, lo=0, count=64):
            return D.at[pl.ds(mo(((z + off + 8) % 8) * 64 + lo, 32), count), :]

        s4 = [wire.slot() for _ in range(2)]
        s3 = [wire.slot() for _ in range(2)]
        s1 = [wire.slot() for _ in range(2)]
        s2 = [wire.slot() for _ in range(2)]
        blocks((4, 0))
        wire.send(part(4, 0, 32), q4.at[0], s4[0], zs[2])
        wire.send(part(4, 32, 32), q4.at[1], s4[1], zs[6])
        blocks((3, 5))
        wire.send(part(3), q3.at[0], s3[0], zs[1])
        wire.send(part(5), q3.at[1], s3[1], zs[7])
        blocks((2, 6))
        blocks((1, 7))
        wire.send(part(1), n1.at[0], s1[0], zs[1])
        wire.send(part(7), n1.at[1], s1[1], zs[7])
        yield
        for n, (off, near, far) in enumerate(((2, 7, 6), (6, 1, 2))):
            wire.recv(q3.at[n], s3[n], zs[near])
            wire.recv(q4.at[n], s4[n], zs[far])
            acc = part(off)
            total = acc[...].astype(F32) + q3[n].astype(F32)
            both = [total[0:32], total[32:64]]
            both[n] = both[n] + q4[n].astype(F32)
            acc[...] = jnp.concatenate(both, axis=0).astype(BF)
            wire.send(acc, n2.at[n], s2[n], zs[off])
        yield
        total = part(0)[...].astype(F32)
        for n in range(2):
            wire.recv(n1.at[n], s1[n], zs[(7, 1)[n]])
            wire.recv(n2.at[n], s2[n], zs[(6, 2)[n]])
            total = total + n1[n].astype(F32) + n2[n].astype(F32)
        tsum[...] = total
        tbf[...] = total.astype(BF)
        ys = {j: wire.slot() for j in (1, 2, 3)}
        for j in (2, 1, 3):
            wire.send(tbf.at[pl.ds(mo(((yh + j) % 4) * 16, 16), 16), :], yb.at[j - 1], ys[j], yhs[j])
        yield
        total = tsum[pl.ds(mo(yh * 16, 16), 16), :]
        for j in (1, 3, 2):
            wire.recv(yb.at[j - 1], ys[j], yhs[4 - j])
            total = total + yb[j - 1].astype(F32)
        result.append(total)
        yield

    def bulk():
        gate_up((3, 5))
        gate_up((4,))
        sq = sq_rounds(SS, SSr)
        next(sq)
        yield

        def blk(off, h):
            return pl.ds(mo(((x + off) % 4) * 64 + h * 32, 32), 32)

        xslot = [[wire.slot() for _ in range(6)] for _ in range(NG)]
        for d in range(8):
            wire.recv(crecv.at[unit_rows(d), :], cslot[d], core)
        for p in range(NG):
            @pl.loop(0, 8)
            def _(i):
                r = pl.ds(mo(i * 32, 32), 32)
                own[r, cols(p)] = (G[pl.ds(mo(i * 64 + c * 32, 32), 32), cols(p)].astype(F32)
                                   + crecv[r, cols(p)].astype(F32)).astype(BF)
            wire.send(own.at[blk(2, 0), cols(p)], fwdp.at[:, cols(p)], xslot[p][0], xs[1])
            wire.send(own.at[blk(2, 1), cols(p)], fwdm.at[:, cols(p)], xslot[p][1], xs[3])
            wire.send(own.at[blk(1, 1), cols(p)], dirp.at[32:64, cols(p)], xslot[p][2], xs[1])
            wire.send(own.at[blk(3, 0), cols(p)], dirm.at[0:32, cols(p)], xslot[p][3], xs[3])
        next(sq)
        yield
        for p in range(NG):
            wire.recv(fwdp.at[:, cols(p)], xslot[p][0], xs[3])
            r = blk(1, 0)
            own[r, cols(p)] = (own[r, cols(p)].astype(F32) + fwdp[:, cols(p)].astype(F32)).astype(BF)
            wire.send(own.at[r, cols(p)], dirp.at[0:32, cols(p)], xslot[p][4], xs[1])
            wire.recv(fwdm.at[:, cols(p)], xslot[p][1], xs[1])
            r = blk(3, 1)
            own[r, cols(p)] = (own[r, cols(p)].astype(F32) + fwdm[:, cols(p)].astype(F32)).astype(BF)
            wire.send(own.at[r, cols(p)], dirm.at[32:64, cols(p)], xslot[p][5], xs[3])
        next(sq)
        yield
        yslot = [wire.slot() for _ in range(NG)]
        for p in range(NG):
            wire.recv(dirp.at[32:64, cols(p)], xslot[p][2], xs[3])
            wire.recv(dirm.at[0:32, cols(p)], xslot[p][3], xs[1])
            wire.recv(dirp.at[0:32, cols(p)], xslot[p][4], xs[3])
            wire.recv(dirm.at[32:64, cols(p)], xslot[p][5], xs[1])

            def xsum(h):
                hr = pl.ds(mo(h * 32, 32), 32)
                return (own[blk(0, h), cols(p)].astype(F32) + dirp[hr, cols(p)].astype(F32)
                        + dirm[hr, cols(p)].astype(F32))
            ysnd[:, cols(p)] = xsum(other).astype(BF)
            wire.send(ysnd.at[:, cols(p)], yrecv.at[:, cols(p)], yslot[p], ydev)
            tot[:, cols(p)] = xsum(mine)
        yield
        scale = scale_of(SSr, (x * 2 + yl) * 128 + c * 32, 32)

        def hrows(off, h):
            return pl.ds(mo(c * 256 + ((x + off) % 4) * 64 + h * 32, 32), 32)

        hy = [wire.slot() for _ in range(NG)]
        hx = [[wire.slot() for _ in range(6)] for _ in range(NG)]
        hc = [wire.slot() for _ in range(NG)]

        def hcols(p):
            lo, w = GROUPS[p]
            return slice(lo, lo + w)

        def hsend(off, h, p, slot, dev):
            same(H.at[hrows(off, h), hcols(p)], slot, dev)

        def hrecv(off, h, p, slot, dev):
            wire.recv(H.at[hrows(off, h), hcols(p)], slot, dev)

        for p in range(NG):
            lo, w = GROUPS[p]
            wire.recv(yrecv.at[:, cols(p)], yslot[p], ydev)
            gate = (tot[:, 2 * lo:2 * lo + w] + yrecv[:, 2 * lo:2 * lo + w].astype(F32)) * scale
            up = (tot[:, 2 * lo + w:2 * lo + 2 * w] + yrecv[:, 2 * lo + w:2 * lo + 2 * w].astype(F32)) * scale
            H[hrows(0, mine), hcols(p)] = act(gate, up)
            hsend(0, mine, p, hy[p], ydev)
            hsend(0, mine, p, hx[p][0], xs[1])
            hsend(0, mine, p, hx[p][1], xs[3])
        yield
        for p in range(NG):
            hrecv(0, other, p, hy[p], ydev)
            hsend(0, other, p, hx[p][2], xs[1])
            hsend(0, other, p, hx[p][3], xs[3])
            hrecv(3, mine, p, hx[p][0], xs[3])
            hsend(3, mine, p, hx[p][4], xs[1])
            hrecv(1, mine, p, hx[p][1], xs[1])
        yield
        for p in range(NG):
            hrecv(3, other, p, hx[p][2], xs[3])
            hrecv(1, other, p, hx[p][3], xs[1])
            hsend(1, other, p, hx[p][5], xs[3])
        yield
        for p in range(NG):
            hrecv(2, mine, p, hx[p][4], xs[3])
            hrecv(2, other, p, hx[p][5], xs[1])
            half = H.at[pl.ds(mo(c * 256, 256), 256), hcols(p)]
            same(half, hc[p], core)
        yield
        for p in range(NG):
            wire.recv(H.at[pl.ds(mo((1 - c) * 256, 256), 256), hcols(p)], hc[p], core)

        def down_blocks(ds):
            units = [pl.ds(mo(cc * 256 + ((z + d) % 8) * 32, 32), 32) for d in ds for cc in (0, 1)]
            both = jnp.concatenate([H[u, :] for u in units], axis=0)
            prod = jnp.dot(both, WD[...], preferred_element_type=F32).astype(BF)
            for n, d in enumerate(ds):
                D[pl.ds(mo(((z + d) % 8) * 64, 64), 64), :] = prod[n * 64:n * 64 + 64]

        delta = []
        for _ in z_reduce(delta, down_blocks):
            if not delta:
                yield
        st[...] = tok_rows() + delta[0]
        yield

    def tok_rows():
        return X[my_rows, :].astype(F32)

    def down_of(n):
        return jnp.dot(H2[n, :, 0:896], WD[...], preferred_element_type=F32)

    def run(*gens):
        for gen in gens:
            next(gen)

    p1, big = packed(0), (bulk() if upto not in (7, 70, 71, 72) else iter(int, 1))
    if upto in (7, 70, 71, 72):
        st[...] = tok_rows()

    def stop(*gens):
        for gen in (gens if upto < 9 else ()):
            for _ in gen:
                pass
        out[...] = XF[0:16, :].astype(BF)
        finish()

    SPEC = {2: 2, 5: 1, 6: 1, 7: 1, 8: 1, 10: 1, 11: 1, 12: 1, 15: 1, 16: 1, 17: 9}
    count = [0]

    def fast(gen):
        next(gen)
        count[0] += 1
        if upto in (0, 7, 70, 71, 72):
            return
        for _ in range(SPEC.get(count[0], 0)):
            if next(big, done) is done:
                break

    for _ in range(5):
        fast(p1)
        if count[0] == 4:
            load_down.wait()
    if upto == 70:
        return stop(big)
    change = []
    total = all_sum(0, down_of(0), change)
    for _ in range(4):
        fast(total)
    XF[...] = XF[...] + change[0]
    if upto == 71:
        return stop(big)
    p2 = packed(1)
    for _ in range(5):
        fast(p2)
    if upto == 72:
        return stop(big)

    total = all_sum(1, down_of(1), change)
    fast(total)
    counts = jnp.sum(flags, axis=1, keepdims=True)
    before = jnp.sum(jnp.where(lax.broadcasted_iota(jnp.int32, (32, 1), 0) < t, counts, 0.0), axis=0, keepdims=True)
    act_row = (RV[...] == 2).astype(F32)
    sub = lax.broadcasted_iota(jnp.int32, (16, 16), 0)
    lane = lax.broadcasted_iota(jnp.int32, (16, 16), 1)
    act_col = jnp.sum(jnp.where(sub == lane, act_row, 0.0), axis=1, keepdims=True)
    place_col = jnp.sum(jnp.where(lane <= sub, act_row, 0.0), axis=1, keepdims=True) - 1.0
    place = jnp.where(act_col > 0.5, before + place_col, -1.0)
    take_rows = jnp.where(place == lax.broadcasted_iota(jnp.int32, (16, 64), 1).astype(F32), 1.0, 0.0).astype(BF)
    for _ in range(3):
        fast(total)
    out[...] = (st[...] + jnp.dot(take_rows, change[1].astype(BF), preferred_element_type=F32)).astype(BF)
    finish()


def body(upto, tokens, norm_gain, gate_weight, up_weight, down_weight, revisit):
    vm = lambda *shape: pltpu.VMEM(shape, BF)
    vf = lambda *shape: pltpu.VMEM(shape, F32)
    vspec, hbm = pl.BlockSpec(memory_space=pltpu.VMEM), pl.BlockSpec(memory_space=pltpu.MemorySpace.HBM)
    scratch = [
        vm(512, 512), vm(512, 1792), vm(896, 512), vf(32, 1, 128), vf(1, 512), pltpu.VMEM((1, 16), jnp.int32),
        vm(512, 1792), vm(256, 1792), vm(256, 1792), vm(32, 1792), vm(32, 1792), vm(64, 1792), vm(64, 1792),
        vm(32, 1792), vm(32, 1792), vf(32, 1792), vm(512, 896),
        vm(512, 512), vm(2, 32, 512), vm(2, 64, 512), vm(2, 64, 512), vm(2, 64, 512),
        vf(64, 512), vm(64, 512), vm(3, 16, 512),
        vf(8, 128), vf(10, 8, 128), vf(2, 8, 128), vf(2, 10, 8, 128), vm(512, 512), vm(128, 512),
        vf(64, 512), vm(2, 64, 512), vm(2, 64, 2048), vm(2, 32, 2048), vm(2, 7, 16, 512), vm(2, 64, 1024),
        vm(2, 128, 256), vm(2, 7, 16, 256), vm(2, 3, 16, 256), vm(2, 16, 256), vm(2, 128, 256),
        vf(16, 512),
        pltpu.SemaphoreType.DMA((12,)), pltpu.SemaphoreType.DMA((320,)), pltpu.SemaphoreType.DMA((320,)),
    ]
    return pl.pallas_call(
        functools.partial(kernel, upto),
        out_shape=jax.ShapeDtypeStruct((16, 512), BF),
        in_specs=[hbm] * 6,
        out_specs=vspec,
        scratch_shapes=scratch,
        compiler_params=pltpu.CompilerParams(
            collective_id=0, has_side_effects=True, vmem_limit_bytes=60 * 1024 * 1024),
        cost_estimate=pl.CostEstimate(flops=2000000000, bytes_accessed=3000000, transcendentals=30000),
        name="two_pass_block",
    )(tokens, norm_gain.reshape(1, 512), revisit.reshape(1, 16), gate_weight, up_weight, down_weight)


def solution(mesh, upto=LAST):
    placed = (P("tp", "section"), P("section"), P("section", "tp"), P("section", "tp"), P("tp", "section"), P("tp"))
    return jax.shard_map(functools.partial(body, upto), mesh=mesh, in_specs=placed,
                         out_specs=P("tp", "section"), check_vma=False)
```

```python
import functools
import jax
import jax.numpy as jnp
from jax import lax
from jax.experimental import pallas as pl
from jax.experimental.pallas import tpu as pltpu
from jax.sharding import PartitionSpec as P

BF, F32 = jnp.bfloat16, jnp.float32
GROUPS = ((0, 256), (256, 256), (512, 256), (768, 128))
FEATURES = 8192.0
EPS = 1e-5
LAST = 99


def mo(value, unit):
    return pl.multiple_of(value, unit)


def eye(rows, lanes, offset=0):
    row = lax.broadcasted_iota(jnp.int32, (rows, lanes), 0)
    lane = lax.broadcasted_iota(jnp.int32, (rows, lanes), 1)
    return lane == row + offset


class Wire:
    def __init__(self, send_sem, recv_sem):
        self.send_sem, self.recv_sem = send_sem, recv_sem
        self.count, self.sent = 0, []

    def slot(self):
        self.count += 1
        return self.count - 1

    def send(self, src, dst, slot, dev):
        copy = pltpu.make_async_remote_copy(
            src_ref=src, dst_ref=dst, send_sem=self.send_sem.at[slot], recv_sem=self.recv_sem.at[slot],
            device_id=dev, device_id_type=pl.DeviceIdType.MESH)
        copy.start()
        self.sent.append(copy)

    def recv(self, dst, slot, dev):
        pltpu.make_async_remote_copy(
            src_ref=dst, dst_ref=dst, send_sem=self.send_sem.at[slot], recv_sem=self.recv_sem.at[slot],
            device_id=dev, device_id_type=pl.DeviceIdType.MESH).wait_recv()

    def drain(self):
        for copy in self.sent:
            copy.wait_send()


def kernel(upto, tok, gain, rev, wg, wu, wd, out,
           X, W, WD, F, GN, RV, G, own, crecv, fwdp, fwdm, dirp, dirm, ysnd, yrecv, tot, H,
           D, q4, q3, n1, n2, tsum, tbf, yb, SS, SSr, S2, S2r, TRI, SPR,
           CH, XF, C, G2, c2r, x2r, H2, PF, zr, z3, yex, ZA, st,
           wsem, send_sem, recv_sem):
    s, t = lax.axis_index("section"), lax.axis_index("tp")
    c, x, yl = s % 2, (s // 2) % 4, s // 8
    z, yh = t // 4, t % 4
    wire = Wire(send_sem, recv_sem)
    mine, other = yl, 1 - yl

    def sec(dc=0, dx=0, dy=0):
        return ((((yl + dy + 2) % 2) * 4 + (x + dx + 4) % 4) * 2 + (c + dc) % 2, t)

    def tpd(dz=0, dh=0):
        return (s, ((z + dz + 8) % 8) * 4 + (yh + dh + 4) % 4)

    core, ydev = sec(dc=1), sec(dy=1)
    xs = {j: sec(dx=j) for j in (1, 2, 3)}
    zs = {j: tpd(dz=j) for j in range(1, 8)}
    ups, downs = zs[1], zs[7]
    yhs = {j: tpd(dh=j) for j in (1, 2, 3)}
    around = [(2, 1), (2, 0), (1, 1), (3, 1), (1, 0), (3, 0), (0, 1)]
    xys = [sec(dx=a, dy=b) for a, b in around]

    loads = []
    for g, (lo, w) in enumerate(GROUPS):
        loads.append(pltpu.make_async_copy(wg.at[:, lo:lo + w], W.at[:, 2 * lo:2 * lo + w], wsem.at[2 * g]))
        loads.append(pltpu.make_async_copy(wu.at[:, lo:lo + w], W.at[:, 2 * lo + w:2 * lo + 2 * w], wsem.at[2 * g + 1]))
    load_down = pltpu.make_async_copy(wd, WD, wsem.at[8])
    my_rows = pl.ds(mo(t * 16, 16), 16)
    small = [pltpu.make_async_copy(tok, X.at[my_rows, :], wsem.at[9]), pltpu.make_async_copy(rev, RV, wsem.at[10]),
             pltpu.make_async_copy(gain, GN, wsem.at[11])]
    for load in small + loads + [load_down]:
        load.start()

    barrier = pltpu.get_barrier_semaphore()
    peers = [core] + list(zs.values()) + list(yhs.values()) + xys
    for peer in peers:
        pl.semaphore_signal(barrier, inc=1, device_id=peer, device_id_type=pl.DeviceIdType.MESH)
    TRI[...] = jnp.where(lax.broadcasted_iota(jnp.int32, (512, 512), 0)
                         <= lax.broadcasted_iota(jnp.int32, (512, 512), 1), 1.0, 0.0).astype(BF)
    SPR[...] = jnp.where(lax.broadcasted_iota(jnp.int32, (128, 512), 1) % 16
                         == lax.broadcasted_iota(jnp.int32, (128, 512), 0), 1.0, 0.0).astype(BF)
    for load in small:
        load.wait()
    flag_row = jnp.where(RV[...] == 2, 1.0, 0.0)
    F[t] = jnp.concatenate([flag_row, jnp.zeros((1, 112), F32)], axis=1)
    pl.semaphore_wait(barrier, len(peers))
    done = object()

    def finish():
        wire.drain()

    def rows(dz, j):
        return X.at[pl.ds(mo(((z + dz + 8) % 8) * 64 + ((yh - j + 4) % 4) * 16, 16), 16), :]

    def frow(dz):
        return F.at[pl.ds(((z + dz + 8) % 8) * 4, 4)]

    def same(ref, slot, dev):
        wire.send(ref, ref, slot, dev)

    fy = {j: wire.slot() for j in (1, 2, 3)}
    fz = {d: wire.slot() for d in range(1, 8)}
    sy = {j: wire.slot() for j in (1, 2, 3)}
    sz = {(d, j): wire.slot() for d in range(1, 8) for j in range(4)}
    for j in (2, 1, 3):
        same(F.at[pl.ds(t, 1)], fy[j], yhs[j])
        same(rows(0, 0), sy[j], yhs[j])

    def spread(j):
        for d in ((2, 6, 1, 7) if 'drrr'[j] == 'r' else (4, 3, 5, 2, 6, 1, 7)):
            same(rows(0, j), sz[d, j], zs[d])

    def relay(j):
        if 'drrr'[j] == 'd':
            wire.recv(rows(-2, j), sz[2, j], zs[6])
            wire.recv(rows(2, j), sz[6, j], zs[2])
            return
        wire.recv(rows(-2, j), sz[2, j], zs[6])
        if j in (0, 1):
            same(rows(-2, j), sz[4, j], zs[2])
        same(rows(-2, j), sz[3, j], zs[1])
        wire.recv(rows(2, j), sz[6, j], zs[2])
        if j in (2, 3):
            same(rows(2, j), sz[4, j], zs[6])
        same(rows(2, j), sz[5, j], zs[7])

    def take(d):
        for j in (0, 1, 3, 2):
            if d == 4:
                wire.recv(rows(4, j), sz[4, j], zs[6] if j in (0, 1) else zs[2])
            else:
                wire.recv(rows(-d, j), sz[d, j], zs[7])
                wire.recv(rows(d, j), sz[8 - d, j], zs[1])

    NG = len(GROUPS)

    def cols(p):
        lo, w = GROUPS[p]
        return slice(2 * lo, 2 * lo + 2 * w)

    cslot = {d: wire.slot() for d in range(8)}
    g = GN[...]

    def half_rows(d, cc):
        return pl.ds(mo(((z + d) % 8) * 64 + cc * 32, 32), 32)

    def unit_rows(d):
        return pl.ds(mo(((z + d) % 8) * 32, 32), 32)

    def gate_up(ds):
        blocks = [pl.ds(mo(((z + d) % 8) * 64, 64), 64) for d in ds]
        v = jnp.concatenate([X[b, :] for b in blocks], axis=0).astype(F32)
        scaled = (v * g).astype(BF)
        col = jnp.sum(v * v, axis=1, keepdims=True)
        for n, d in enumerate(ds):
            SS[pl.ds((z + d) % 8, 1), :] = jnp.sum(
                jnp.where(eye(64, 128), col[n * 64:n * 64 + 64], 0.0), axis=0, keepdims=True)
        for p in range(NG):
            prod = jnp.dot(scaled, W[:, cols(p)], preferred_element_type=F32).astype(BF)
            for n, b in enumerate(blocks):
                G[b, cols(p)] = prod[n * 64:n * 64 + 64]
        for d in ds:
            wire.send(G.at[half_rows(d, 1 - c), :], crecv.at[unit_rows(d), :], cslot[d], core)

    def pair_sum(d):
        r = unit_rows(d)
        wire.recv(crecv.at[r, :], cslot[d], core)
        own[r, :] = (G[half_rows(d, c), :].astype(F32) + crecv[r, :].astype(F32)).astype(BF)

    spread(0)
    for j in (1, 3):
        wire.recv(rows(0, j), sy[j], yhs[4 - j])
        spread(j)
    relay(0)
    for j in (1, 2, 3):
        wire.recv(F.at[pl.ds(z * 4 + (yh - j + 4) % 4, 1)], fy[j], yhs[4 - j])
    for d in (2, 6, 1, 7):
        same(frow(0), fz[d], zs[d])
    wire.recv(rows(0, 2), sy[2], yhs[2])
    spread(2)
    relay(1)
    relay(3)
    for load in loads:
        load.wait()
    if upto not in (0, 7, 70, 71, 72):
        gate_up((0,))
    wire.recv(frow(-2), fz[2], zs[6])
    same(frow(-2), fz[4], zs[2])
    same(frow(-2), fz[3], zs[1])
    wire.recv(frow(2), fz[6], zs[2])
    same(frow(2), fz[5], zs[7])
    relay(2)
    take(1)
    if upto not in (0, 7, 70, 71, 72):
        gate_up((1, 7))
        pair_sum(0)
        gate_up((2, 6))
        pair_sum(1)
        pair_sum(7)
    wire.recv(frow(-1), fz[1], zs[7])
    wire.recv(frow(1), fz[7], zs[1])
    wire.recv(frow(-3), fz[3], zs[7])
    wire.recv(frow(3), fz[5], zs[1])
    wire.recv(frow(4), fz[4], zs[6])
    flags = F[...].reshape(32, 128)
    lanes = jnp.dot(flags.astype(BF), SPR[...], preferred_element_type=F32)
    owner = lax.broadcasted_iota(jnp.int32, (32, 512), 1) // 16
    unit = lax.broadcasted_iota(jnp.int32, (32, 512), 0)
    active = jnp.sum(jnp.where(unit == owner, lanes, 0.0), axis=0, keepdims=True)
    upto_here = jnp.dot(jnp.broadcast_to(active, (16, 512)).astype(BF), TRI[...], preferred_element_type=F32)[0:1, :]
    want = lax.broadcasted_iota(jnp.int32, (64, 512), 0).astype(F32)
    goal = jnp.where(active > 0.5, upto_here - 1.0, -1.0)
    choose = jnp.where(goal == want, 1.0, 0.0).astype(BF)
    CH[...] = choose
    take(3)
    take(4)
    if upto < 1:
        load_down.wait()
        out[...] = X[my_rows, :]
        return finish()

    XF[...] = jnp.dot(CH[...], X[...], preferred_element_type=F32)

    def sq_rounds(ss, rr):
        slots = [wire.slot() for _ in range(8)]
        wire.send(ss, rr.at[0], slots[0], core)
        yield
        wire.recv(rr.at[0], slots[0], core)
        rr[8] = ss[...] + rr[0]
        for q in range(7):
            wire.send(rr.at[8], rr.at[q + 1], slots[q + 1], xys[q])
        yield
        total = rr[8]
        for q in range(7):
            wire.recv(rr.at[q + 1], slots[q + 1], sec(dx=-around[q][0], dy=around[q][1]))
            total = total + rr[q + 1]
        rr[9] = total
        yield

    def scale_of(rr, first, count):
        line = rr[9, pl.ds(first // 128, 1), :]
        picked = jnp.where(eye(count, 128, first % 128), line, 0.0)
        return lax.rsqrt(jnp.sum(picked, axis=1, keepdims=True) / FEATURES + EPS)

    def act(gate, up):
        return (gate / (1.0 + jnp.exp(-gate)) * up).astype(BF)

    def packed(n):
        v = XF[...]
        C[n] = (v * g).astype(BF)
        col = jnp.sum(v * v, axis=1, keepdims=True)
        s2 = S2.at[n]
        s2[...] = jnp.zeros((8, 128), F32)
        s2[0:1, :] = jnp.sum(jnp.where(eye(64, 128), col, 0.0), axis=0, keepdims=True)
        g2, h2all = G2.at[n], H2.at[n]
        away = pl.ds(mo((1 - c) * 32, 32), 32)
        core_rows = pl.ds(mo(c * 32, 32), 32)
        group = [wire.slot() for _ in range(NG)]
        for p in range(NG):
            lo, w = GROUPS[p]
            prod = jnp.dot(C[n], W[:, cols(p)], preferred_element_type=F32).astype(BF)
            g2[:, 512 * p:512 * p + w] = prod[:, 0:w]
            g2[:, 512 * p + 256:512 * p + 256 + w] = prod[:, w:2 * w]
            if w < 256:
                g2[:, 512 * p + w:512 * p + 256] = jnp.zeros((64, 256 - w), BF)
                g2[:, 512 * p + 256 + w:512 * p + 512] = jnp.zeros((64, 256 - w), BF)
            wire.send(g2.at[away, 512 * p:512 * p + 512], c2r.at[n, :, 512 * p:512 * p + 512], group[p], core)
        sq = sq_rounds(s2, S2r.at[n])
        next(sq)
        yield
        for p in range(NG):
            wide = slice(512 * p, 512 * p + 512)
            wire.recv(c2r.at[n, :, wide], group[p], core)
            g2[core_rows, wide] = (g2[core_rows, wide].astype(F32) + c2r[n, :, wide].astype(F32)).astype(BF)

        def block(dx, dy):
            return g2.at[pl.ds(mo(c * 32 + ((yl + dy) % 2) * 16, 16), 16), pl.ds(mo(((x + dx) % 4) * 512, 512), 512)]
        slots = [wire.slot() for _ in range(7)]
        for q, (dx, dy) in enumerate(around):
            wire.send(block(dx, dy), x2r.at[n, q], slots[q], xys[q])
        next(sq)
        yield
        total = block(0, 0)[...].astype(F32)
        for q, (dx, dy) in enumerate(around):
            wire.recv(x2r.at[n, q], slots[q], sec(dx=-dx, dy=dy))
            total = total + x2r[n, q].astype(F32)
        next(sq)
        total = total * scale_of(S2r.at[n], c * 32 + yl * 16, 16)

        def hid(dx, dy):
            return h2all.at[pl.ds(mo(c * 32 + ((yl + dy) % 2) * 16, 16), 16), pl.ds(mo(((x + dx + 4) % 4) * 256, 256), 256)]
        hid(0, 0)[...] = act(total[:, 0:256], total[:, 256:512])
        slots = [wire.slot() for _ in range(7)]
        for q in range(7):
            same(hid(0, 0), slots[q], xys[q])
        yield
        for q, (dx, dy) in enumerate(around):
            wire.recv(hid(-dx, dy), slots[q], sec(dx=-dx, dy=dy))
        slot = wire.slot()
        same(h2all.at[core_rows, :], slot, core)
        yield
        wire.recv(h2all.at[pl.ds(mo((1 - c) * 32, 32), 32), :], slot, core)
        yield

    def all_sum(n, prod, result):
        folded = jnp.concatenate([prod[:, 0:256].reshape(8, 8, 256), prod[:, 256:512].reshape(8, 8, 256)], axis=1)
        pf, za = PF.at[n], ZA.at[n]
        pf[...] = folded.reshape(128, 256).astype(BF)

        def blk16(ref, dz):
            return ref.at[pl.ds(mo(((z + dz + 8) % 8) * 16, 16), 16), :]
        slots = {d: wire.slot() for d in range(1, 8)}
        for d in (4, 3, 5, 2, 6, 1, 7):
            wire.send(blk16(pf, d), zr.at[n, d - 1], slots[d], zs[d])
        yield
        total = blk16(pf, 0)[...].astype(F32)
        for d in (1, 7, 2, 6, 3, 5, 4):
            wire.recv(zr.at[n, d - 1], slots[d], zs[8 - d])
            total = total + zr[n, d - 1].astype(F32)
        yex[n] = total.astype(BF)
        ys = {j: wire.slot() for j in (1, 2, 3)}
        for j in (2, 1, 3):
            wire.send(yex.at[n], z3.at[n, j - 1], ys[j], yhs[j])
        yield
        total = yex[n].astype(F32)
        for j in (1, 3, 2):
            wire.recv(z3.at[n, j - 1], ys[j], yhs[4 - j])
            total = total + z3[n, j - 1].astype(F32)
        blk16(za, 0)[...] = total.astype(BF)
        zg = {d: wire.slot() for d in range(1, 8)}
        for d in (4, 3, 5, 2, 6, 1, 7):
            same(blk16(za, 0), zg[d], zs[d])
        yield
        for d in (1, 7, 2, 6, 3, 5, 4):
            wire.recv(blk16(za, -d), zg[d], zs[8 - d])
        got = za[...].astype(F32).reshape(8, 16, 256)
        result.append(jnp.concatenate(
            [got[:, 0:8, :].reshape(64, 256), got[:, 8:16, :].reshape(64, 256)], axis=1))
        yield

    def z_reduce(result, blocks):
        def part(off, lo=0, count=64):
            return D.at[pl.ds(mo(((z + off + 8) % 8) * 64 + lo, 32), count), :]

        s4 = [wire.slot() for _ in range(2)]
        s3 = [wire.slot() for _ in range(2)]
        s1 = [wire.slot() for _ in range(2)]
        s2 = [wire.slot() for _ in range(2)]
        blocks((4, 0))
        wire.send(part(4, 0, 32), q4.at[0], s4[0], zs[2])
        wire.send(part(4, 32, 32), q4.at[1], s4[1], zs[6])
        blocks((3, 5))
        wire.send(part(3), q3.at[0], s3[0], zs[1])
        wire.send(part(5), q3.at[1], s3[1], zs[7])
        blocks((2, 6))
        blocks((1, 7))
        wire.send(part(1), n1.at[0], s1[0], zs[1])
        wire.send(part(7), n1.at[1], s1[1], zs[7])
        yield
        for n, (off, near, far) in enumerate(((2, 7, 6), (6, 1, 2))):
            wire.recv(q3.at[n], s3[n], zs[near])
            wire.recv(q4.at[n], s4[n], zs[far])
            acc = part(off)
            total = acc[...].astype(F32) + q3[n].astype(F32)
            both = [total[0:32], total[32:64]]
            both[n] = both[n] + q4[n].astype(F32)
            acc[...] = jnp.concatenate(both, axis=0).astype(BF)
            wire.send(acc, n2.at[n], s2[n], zs[off])
        yield
        total = part(0)[...].astype(F32)
        for n in range(2):
            wire.recv(n1.at[n], s1[n], zs[(7, 1)[n]])
            wire.recv(n2.at[n], s2[n], zs[(6, 2)[n]])
            total = total + n1[n].astype(F32) + n2[n].astype(F32)
        tsum[...] = total
        tbf[...] = total.astype(BF)
        ys = {j: wire.slot() for j in (1, 2, 3)}
        for j in (2, 1, 3):
            wire.send(tbf.at[pl.ds(mo(((yh + j) % 4) * 16, 16), 16), :], yb.at[j - 1], ys[j], yhs[j])
        yield
        total = tsum[pl.ds(mo(yh * 16, 16), 16), :]
        for j in (1, 3, 2):
            wire.recv(yb.at[j - 1], ys[j], yhs[4 - j])
            total = total + yb[j - 1].astype(F32)
        result.append(total)
        yield

    def bulk():
        gate_up((3, 5))
        gate_up((4,))
        sq = sq_rounds(SS, SSr)
        next(sq)
        yield

        def blk(off, h):
            return pl.ds(mo(((x + off) % 4) * 64 + h * 32, 32), 32)

        xslot = [[wire.slot() for _ in range(6)] for _ in range(NG)]
        for d in (2, 6, 3, 5, 4):
            pair_sum(d)
        for p in range(NG):
            wire.send(own.at[blk(2, 0), cols(p)], fwdp.at[:, cols(p)], xslot[p][0], xs[1])
            wire.send(own.at[blk(2, 1), cols(p)], fwdm.at[:, cols(p)], xslot[p][1], xs[3])
            wire.send(own.at[blk(1, 1), cols(p)], dirp.at[32:64, cols(p)], xslot[p][2], xs[1])
            wire.send(own.at[blk(3, 0), cols(p)], dirm.at[0:32, cols(p)], xslot[p][3], xs[3])
        next(sq)
        yield
        for p in range(NG):
            wire.recv(fwdp.at[:, cols(p)], xslot[p][0], xs[3])
            r = blk(1, 0)
            own[r, cols(p)] = (own[r, cols(p)].astype(F32) + fwdp[:, cols(p)].astype(F32)).astype(BF)
            wire.send(own.at[r, cols(p)], dirp.at[0:32, cols(p)], xslot[p][4], xs[1])
            wire.recv(fwdm.at[:, cols(p)], xslot[p][1], xs[1])
            r = blk(3, 1)
            own[r, cols(p)] = (own[r, cols(p)].astype(F32) + fwdm[:, cols(p)].astype(F32)).astype(BF)
            wire.send(own.at[r, cols(p)], dirm.at[32:64, cols(p)], xslot[p][5], xs[3])
        next(sq)
        yield
        yslot = [wire.slot() for _ in range(NG)]
        for p in range(NG):
            wire.recv(dirp.at[32:64, cols(p)], xslot[p][2], xs[3])
            wire.recv(dirm.at[0:32, cols(p)], xslot[p][3], xs[1])
            wire.recv(dirp.at[0:32, cols(p)], xslot[p][4], xs[3])
            wire.recv(dirm.at[32:64, cols(p)], xslot[p][5], xs[1])

            def xsum(h):
                hr = pl.ds(mo(h * 32, 32), 32)
                return (own[blk(0, h), cols(p)].astype(F32) + dirp[hr, cols(p)].astype(F32)
                        + dirm[hr, cols(p)].astype(F32))
            ysnd[:, cols(p)] = xsum(other).astype(BF)
            wire.send(ysnd.at[:, cols(p)], yrecv.at[:, cols(p)], yslot[p], ydev)
            tot[:, cols(p)] = xsum(mine)
        yield
        scale = scale_of(SSr, (x * 2 + yl) * 128 + c * 32, 32)

        def hrows(off, h):
            return pl.ds(mo(c * 256 + ((x + off) % 4) * 64 + h * 32, 32), 32)

        hy = [wire.slot() for _ in range(NG)]
        hx = [[wire.slot() for _ in range(6)] for _ in range(NG)]
        hc = [wire.slot() for _ in range(NG)]

        def hcols(p):
            lo, w = GROUPS[p]
            return slice(lo, lo + w)

        def hsend(off, h, p, slot, dev):
            same(H.at[hrows(off, h), hcols(p)], slot, dev)

        def hrecv(off, h, p, slot, dev):
            wire.recv(H.at[hrows(off, h), hcols(p)], slot, dev)

        for p in range(NG):
            lo, w = GROUPS[p]
            wire.recv(yrecv.at[:, cols(p)], yslot[p], ydev)
            gate = (tot[:, 2 * lo:2 * lo + w] + yrecv[:, 2 * lo:2 * lo + w].astype(F32)) * scale
            up = (tot[:, 2 * lo + w:2 * lo + 2 * w] + yrecv[:, 2 * lo + w:2 * lo + 2 * w].astype(F32)) * scale
            H[hrows(0, mine), hcols(p)] = act(gate, up)
            hsend(0, mine, p, hy[p], ydev)
            hsend(0, mine, p, hx[p][0], xs[1])
            hsend(0, mine, p, hx[p][1], xs[3])
        yield
        for p in range(NG):
            hrecv(0, other, p, hy[p], ydev)
            hsend(0, other, p, hx[p][2], xs[1])
            hsend(0, other, p, hx[p][3], xs[3])
            hrecv(3, mine, p, hx[p][0], xs[3])
            hsend(3, mine, p, hx[p][4], xs[1])
            hrecv(1, mine, p, hx[p][1], xs[1])
        yield
        for p in range(NG):
            hrecv(3, other, p, hx[p][2], xs[3])
            hrecv(1, other, p, hx[p][3], xs[1])
            hsend(1, other, p, hx[p][5], xs[3])
        yield
        for p in range(NG):
            hrecv(2, mine, p, hx[p][4], xs[3])
            hrecv(2, other, p, hx[p][5], xs[1])
            half = H.at[pl.ds(mo(c * 256, 256), 256), hcols(p)]
            same(half, hc[p], core)
        yield
        for p in range(NG):
            wire.recv(H.at[pl.ds(mo((1 - c) * 256, 256), 256), hcols(p)], hc[p], core)

        def down_blocks(ds):
            units = [pl.ds(mo(cc * 256 + ((z + d) % 8) * 32, 32), 32) for d in ds for cc in (0, 1)]
            both = jnp.concatenate([H[u, :] for u in units], axis=0)
            prod = jnp.dot(both, WD[...], preferred_element_type=F32).astype(BF)
            for n, d in enumerate(ds):
                D[pl.ds(mo(((z + d) % 8) * 64, 64), 64), :] = prod[n * 64:n * 64 + 64]

        delta = []
        for _ in z_reduce(delta, down_blocks):
            if not delta:
                yield
        st[...] = tok_rows() + delta[0]
        yield

    def tok_rows():
        return X[my_rows, :].astype(F32)

    def down_of(n):
        return jnp.dot(H2[n, :, 0:896], WD[...], preferred_element_type=F32)

    def run(*gens):
        for gen in gens:
            next(gen)

    p1, big = packed(0), (bulk() if upto not in (7, 70, 71, 72) else iter(int, 1))
    if upto in (7, 70, 71, 72):
        st[...] = tok_rows()

    def stop(*gens):
        for gen in (gens if upto < 9 else ()):
            for _ in gen:
                pass
        out[...] = XF[0:16, :].astype(BF)
        finish()

    SPEC = {2: 2, 4: 1, 6: 1, 7: 1, 8: 1, 9: 1, 11: 1, 12: 1, 15: 1, 16: 1, 17: 9}
    count = [0]

    def fast(gen):
        next(gen)
        count[0] += 1
        if upto in (0, 7, 70, 71, 72):
            return
        for _ in range(SPEC.get(count[0], 0)):
            if next(big, done) is done:
                break

    for _ in range(5):
        fast(p1)
        if count[0] == 4:
            load_down.wait()
    if upto == 70:
        return stop(big)
    change = []
    total = all_sum(0, down_of(0), change)
    for _ in range(4):
        fast(total)
    XF[...] = XF[...] + change[0]
    if upto == 71:
        return stop(big)
    p2 = packed(1)
    for _ in range(5):
        fast(p2)
    if upto == 72:
        return stop(big)

    total = all_sum(1, down_of(1), change)
    fast(total)
    counts = jnp.sum(flags, axis=1, keepdims=True)
    before = jnp.sum(jnp.where(lax.broadcasted_iota(jnp.int32, (32, 1), 0) < t, counts, 0.0), axis=0, keepdims=True)
    act_row = (RV[...] == 2).astype(F32)
    sub = lax.broadcasted_iota(jnp.int32, (16, 16), 0)
    lane = lax.broadcasted_iota(jnp.int32, (16, 16), 1)
    act_col = jnp.sum(jnp.where(sub == lane, act_row, 0.0), axis=1, keepdims=True)
    place_col = jnp.sum(jnp.where(lane <= sub, act_row, 0.0), axis=1, keepdims=True) - 1.0
    place = jnp.where(act_col > 0.5, before + place_col, -1.0)
    take_rows = jnp.where(place == lax.broadcasted_iota(jnp.int32, (16, 64), 1).astype(F32), 1.0, 0.0).astype(BF)
    for _ in range(3):
        fast(total)
    out[...] = (st[...] + jnp.dot(take_rows, change[1].astype(BF), preferred_element_type=F32)).astype(BF)
    finish()


def body(upto, tokens, norm_gain, gate_weight, up_weight, down_weight, revisit):
    vm = lambda *shape: pltpu.VMEM(shape, BF)
    vf = lambda *shape: pltpu.VMEM(shape, F32)
    vspec, hbm = pl.BlockSpec(memory_space=pltpu.VMEM), pl.BlockSpec(memory_space=pltpu.MemorySpace.HBM)
    scratch = [
        vm(512, 512), vm(512, 1792), vm(896, 512), vf(32, 1, 128), vf(1, 512), pltpu.VMEM((1, 16), jnp.int32),
        vm(512, 1792), vm(256, 1792), vm(256, 1792), vm(32, 1792), vm(32, 1792), vm(64, 1792), vm(64, 1792),
        vm(32, 1792), vm(32, 1792), vf(32, 1792), vm(512, 896),
        vm(512, 512), vm(2, 32, 512), vm(2, 64, 512), vm(2, 64, 512), vm(2, 64, 512),
        vf(64, 512), vm(64, 512), vm(3, 16, 512),
        vf(8, 128), vf(10, 8, 128), vf(2, 8, 128), vf(2, 10, 8, 128), vm(512, 512), vm(128, 512),
        vm(64, 512), vf(64, 512), vm(2, 64, 512), vm(2, 64, 2048), vm(2, 32, 2048), vm(2, 7, 16, 512), vm(2, 64, 1024),
        vm(2, 128, 256), vm(2, 7, 16, 256), vm(2, 3, 16, 256), vm(2, 16, 256), vm(2, 128, 256),
        vf(16, 512),
        pltpu.SemaphoreType.DMA((12,)), pltpu.SemaphoreType.DMA((320,)), pltpu.SemaphoreType.DMA((320,)),
    ]
    return pl.pallas_call(
        functools.partial(kernel, upto),
        out_shape=jax.ShapeDtypeStruct((16, 512), BF),
        in_specs=[hbm] * 6,
        out_specs=vspec,
        scratch_shapes=scratch,
        compiler_params=pltpu.CompilerParams(
            collective_id=0, has_side_effects=True, vmem_limit_bytes=60 * 1024 * 1024),
        cost_estimate=pl.CostEstimate(flops=2000000000, bytes_accessed=3000000, transcendentals=30000),
        name="two_pass_block",
    )(tokens, norm_gain.reshape(1, 512), revisit.reshape(1, 16), gate_weight, up_weight, down_weight)


def solution(mesh, upto=LAST):
    placed = (P("tp", "section"), P("section"), P("section", "tp"), P("section", "tp"), P("tp", "section"), P("tp"))
    return jax.shard_map(functools.partial(body, upto), mesh=mesh, in_specs=placed,
                         out_specs=P("tp", "section"), check_vma=False)
```
